32 devices in a mesh: wide: 8 (over y, x, core), narrow: 4 (over z).
Axes of the slice: x: 2, y: 2, z: 4, core: 2. Of those that a mesh axis runs over, the one named last changes fastest.
Arguments:
- thinker_rows: bfloat16 [8, 4, 3, 2, 128, 2048], P('wide', 'narrow'), may hold values from -6 to 6
- codec_ids: int32 [8, 4, 3, 2, 128], P('wide', 'narrow'), may hold values from 0 to 2047
- block_lengths: int32 [8, 4, 3, 2], P('wide', 'narrow'), may hold values from 1 to 128
- chosen_label: int32 [8, 4, 3], P('wide', 'narrow'), may hold values from 0 to 1
- ref_logratio: float32 [8, 4, 3], P('wide', 'narrow'), may hold values from -6 to 6
- pair_count: int32 [8, 4], P('wide', 'narrow'), may hold values from 1 to 3, as said below
- proj_weight: bfloat16 [2048, 1024], P('narrow'), may hold values from -0.125 to 0.125
- norm_gain: bfloat16 [1024], P('narrow'), may hold values from 0.25 to 1.75
- head_weight: bfloat16 [1024, 2048], P('narrow')
Outputs:
- loss: float32 [], replicated
- grad_head: float32 [1024, 2048], P('narrow')
- grad_gain: float32 [1024], P('narrow')
The draws below stay inside these ranges and needn't reach their ends.
Inputs may be any that keep to these rules, and one draw needn't show every extreme that they name: `pair_count`: owners are ordered with the wide index slowest; the counts sum to 64; the sum of the counts of owners below owner i lies between i * 2 and i * 2 + 1; some owner holds 3 live pairs.
All inputs are finite; a program needn't handle non-finite values.
Results may differ from the reference program's by a relative error of at most 0.017.
The reference program's roundings to bfloat16 on the way (of `projected`, `normed` and `dlogits`) count: a program that leaves them out, or rounds other values in their place, can miss the bound.
Values may be sent and summed in bfloat16 or wider, within the bound.
A program may use at most 64 MiB of HBM per device.

```python
import jax
import jax.numpy as jnp
from jax import lax

TW = 2048
D = 1024
V = 2048
FRAMES = 128
H = 2
SLOTS = 3
PAIRS = 64
N_WIDE = 8
N_NARROW = 4


def draw_pair_count(key, part):
    owners = N_WIDE * N_NARROW
    first_key = jax.random.fold_in(key, 11)
    second_key = jax.random.fold_in(key, 12)
    drift = jax.random.randint(first_key, (owners + 1,), 0, H)
    marked = jax.random.randint(second_key, (), 1, owners)
    drift = drift.at[marked].set(H - 1)
    drift = drift.at[marked - 1].set(0)
    drift = drift.at[0].set(0)
    drift = drift.at[owners].set(0)
    return (H + drift[1:] - drift[:-1]).astype(jnp.int32).reshape(N_WIDE, N_NARROW)


def draw_head_weight(key, part):
    values = jax.random.normal(jax.random.fold_in(key, 21), (D, V), jnp.float32) / jnp.sqrt(jnp.float32(D))
    return values.astype(jnp.bfloat16)


def place_ends(entries, rng, smallest, largest):
    longest = entries.shape.index(max(entries.shape))
    spots = []
    for shift in (0, 1):
        where = [jax.random.randint(jax.random.fold_in(rng, axis), (), 0, length) for axis, length in enumerate(entries.shape)]
        where[longest] = (where[longest] + shift) % entries.shape[longest]
        spots.append(tuple(where))
    return entries.at[spots[0]].set(smallest).at[spots[1]].set(largest)


def shard_levels(rng, extent, pieces, least, largest):
    loudness = 1.0
    for position, blocks in pieces:
        draws = jax.random.uniform(jax.random.fold_in(jax.random.fold_in(rng, 6), position), (blocks,), jnp.float32, least / len(pieces), largest / len(pieces))
        loudness = loudness * jnp.repeat(jnp.exp(draws), extent[position] // blocks).reshape((-1,) + (1,) * (len(extent) - 1 - position))
    return loudness


def noise(rng, dims, scale, reach, shards=(), kind=jnp.bfloat16):
    drawn = scale * jax.random.normal(rng, dims, jnp.float32)
    if shards:
        drawn = drawn * shard_levels(rng, dims, shards, -0.22, 0.18)
    return jnp.clip(drawn, -reach, reach).astype(kind)


def setup_inputs(seed: int = 0) -> dict:
    key_of = jax.random.split(jax.random.key(seed), 10)
    return {
        "thinker_rows": noise(key_of[0], (N_WIDE, N_NARROW, SLOTS, 2, FRAMES, TW), 1.0, 6.0, ((0, 8), (1, 4))),
        "codec_ids": place_ends(jax.random.randint(key_of[1], (N_WIDE, N_NARROW, SLOTS, 2, FRAMES), 0, V), jax.random.fold_in(key_of[1], 1), 0, V - 1).astype(jnp.int32),
        "block_lengths": place_ends(jax.random.randint(key_of[2], (N_WIDE, N_NARROW, SLOTS, 2), 1, FRAMES + 1), jax.random.fold_in(key_of[2], 1), 1, FRAMES).astype(jnp.int32),
        "chosen_label": place_ends(jax.random.randint(key_of[3], (N_WIDE, N_NARROW, SLOTS), 0, 2), jax.random.fold_in(key_of[3], 1), 0, 1).astype(jnp.int32),
        "ref_logratio": noise(key_of[4], (N_WIDE, N_NARROW, SLOTS), 1.0, 6.0, ((0, 8), (1, 4)), jnp.float32),
        "pair_count": draw_pair_count(jax.random.fold_in(key_of[9], 71), 0),
        "proj_weight": noise(key_of[6], (TW, D), TW ** -0.5, 0.125, ((0, 4),)),
        "norm_gain": jnp.clip(1.0 + 0.15 * jax.random.normal(key_of[7], (D,), jnp.float32), 0.25, 1.75).astype(jnp.bfloat16),
        "head_weight": draw_head_weight(jax.random.fold_in(key_of[9], 71), 0),
    }


norm_eps = 1e-06
margin_scale = 2.0

def forward_terms(projected, codes, lengths, live_pairs, gain_full, head_full):
    pairs = codes.shape[0]
    frames = codes.shape[2]
    flat = projected.astype(jnp.float32)
    inverse = lax.rsqrt(lax.optimization_barrier(jnp.mean(flat * flat, axis=1, keepdims=True)) + norm_eps)
    normed = (flat * inverse * gain_full.astype(jnp.float32)).astype(jnp.bfloat16)
    logits = jnp.dot(normed, head_full, preferred_element_type=jnp.float32)
    highest = lax.optimization_barrier(jnp.max(logits, axis=1, keepdims=True))
    log_total = highest + jnp.log(lax.optimization_barrier(jnp.sum(jnp.exp(logits - highest), axis=1, keepdims=True)))
    probs = jnp.exp(logits - log_total)
    target = (lax.broadcasted_iota(jnp.int32, logits.shape, 1) == codes.reshape(-1, 1)).astype(jnp.float32)
    token_logp = lax.optimization_barrier(jnp.sum(target * logits, axis=1)) - log_total[:, 0]
    frame_index = jnp.arange(frames, dtype=jnp.int32)
    valid = ((frame_index[None, None, :] < lengths[:, :, None]) & live_pairs[:, None, None]).astype(jnp.float32)
    partial_value = lax.optimization_barrier(jnp.sum(token_logp.reshape(pairs, 2, frames) * valid, axis=2))
    return (normed, flat, inverse, probs, target, valid, partial_value)

def backward_terms(scores, lengths, labels, ratios, live_pairs, normed, flat, inverse, probs, target, valid, head_full):
    length_f = lengths.astype(jnp.float32)
    score = scores / length_f
    first = labels == 0
    chosen = jnp.where(first, score[:, 0], score[:, 1])
    rejected = jnp.where(first, score[:, 1], score[:, 0])
    margin = margin_scale * (chosen - rejected - ratios)
    live_f = live_pairs.astype(jnp.float32)
    loss_part = jnp.sum(jax.nn.softplus(-margin) * live_f)
    slope = -jax.nn.sigmoid(-margin) * live_f
    weight_first = jnp.where(first, margin_scale * slope, -margin_scale * slope)
    block_weight = jnp.stack([weight_first, -weight_first], axis=1) / length_f
    coeff = (block_weight[:, :, None] * valid).reshape(-1, 1)
    dlogits = (coeff * (target - probs)).astype(jnp.bfloat16)
    head_term = jnp.dot(normed.T, dlogits, preferred_element_type=jnp.float32)
    dnormed = jnp.dot(dlogits, head_full.T, preferred_element_type=jnp.float32)
    gain_term = lax.optimization_barrier(jnp.sum(dnormed * flat * inverse, axis=0))
    return (loss_part, head_term, gain_term)

def reference(thinker_rows, codec_ids, block_lengths, chosen_label, ref_logratio, pair_count, proj_weight, norm_gain, head_weight):
    owners = N_WIDE * N_NARROW
    counts = pair_count.reshape(owners)
    live = jnp.arange(SLOTS, dtype=jnp.int32)[None, :] < counts[:, None]

    def one_owner(carry, items):
        rows, codes, lengths, labels, ratios, live_pairs = items
        projected = jnp.dot(rows.reshape(-1, TW), proj_weight, preferred_element_type=jnp.float32).astype(jnp.bfloat16)
        normed, flat, inverse, probs, target, valid, partial_value = forward_terms(projected, codes, lengths, live_pairs, norm_gain, head_weight)
        loss_part, head_term, gain_term = backward_terms(partial_value, lengths, labels, ratios, live_pairs, normed, flat, inverse, probs, target, valid, head_weight)
        return ((carry[0] + loss_part, carry[1] + head_term, carry[2] + gain_term), None)
    start = (jnp.zeros((), jnp.float32), jnp.zeros((D, V), jnp.float32), jnp.zeros((D,), jnp.float32))
    items = (thinker_rows.reshape(owners, SLOTS, 2, FRAMES, TW), codec_ids.reshape(owners, SLOTS, 2, FRAMES), block_lengths.reshape(owners, SLOTS, 2), chosen_label.reshape(owners, SLOTS), ref_logratio.reshape(owners, SLOTS), live)
    totals, unused = lax.scan(one_owner, start, items)
    return (totals[0] / PAIRS, totals[1], totals[2])
```

```python
import functools

import jax
import jax.numpy as jnp
from jax import lax
from jax.experimental import pallas as pl
from jax.experimental.pallas import tpu as pltpu
from jax.sharding import PartitionSpec as P

norm_eps = 1e-06
margin_scale = 2.0
f32 = jnp.float32
bf16 = jnp.bfloat16


def plane_of(wide):
    chips = wide // 2
    rows = 1
    while (rows * 2) * (rows * 2) <= chips:
        rows *= 2
    return rows, chips // rows


def spread_count(nx, ny):
    return 2 * (nx - 1) + 2 * (ny - 1) + 2 * (nx - 1) * (ny - 1) + 1


def copy_count(nx, ny, nz):
    weights = 2 * (nz - 1) * (2 + spread_count(nx, ny)) + (nz - 1)
    sums = nz * (1 + 2 * (nx - 1) + 2 * (ny - 1)) + (nz - 1)
    small = 1 + (nx - 1) + (ny - 1) + (nz - 1)
    return weights + sums + spread_count(nx, ny) + small


def kernel(
    ny, nx, nz, slots, frames, width, dim, vocab, pair_total,
    lengths, labels, counts, ratios,
    rows_in, codes, proj_in, gain_in, head_in,
    loss_out, grad_out, gain_out,
    rows, proj, head, gains, acc, projected, inverse, normed, logits, dlogits,
    term, r1, s1, ra0, ra1, s2a, s2b, rb0, rb1, s3, r3, gather,
    small, sum_c, sum_x, sum_y, sum_z,
    local_sem, send_sem, recv_sem,
):
    w = lax.axis_index("wide")
    z = lax.axis_index("narrow")
    core = lax.rem(w, 2)
    chip = lax.div(w, 2)
    x = lax.rem(chip, nx)
    y = lax.div(chip, nx)
    pair_rows = 2 * frames
    total_rows = slots * pair_rows

    def wide_at(yy, xx, cc):
        return (yy * nx + xx) * 2 + cc

    def shift(i, d, n):
        return lax.rem(i + d, n)

    def x_peer(d):
        return {"wide": wide_at(y, shift(x, d, nx), core), "narrow": z}

    def y_peer(d):
        return {"wide": wide_at(shift(y, d, ny), x, core), "narrow": z}

    def z_peer(d):
        return {"wide": w, "narrow": shift(z, d, nz)}

    mate = {"wide": wide_at(y, x, 1 - core), "narrow": z}
    peers = [mate]
    peers += [x_peer(d) for d in range(1, nx)]
    peers += [y_peer(d) for d in range(1, ny)]
    peers += [z_peer(d) for d in range(1, nz)]

    started = []

    def send(src, dst, device):
        at = len(started)
        copy = pltpu.make_async_remote_copy(
            src_ref=src,
            dst_ref=dst,
            send_sem=send_sem.at[at],
            recv_sem=recv_sem.at[at],
            device_id=device,
            device_id_type=pl.DeviceIdType.MESH,
        )
        copy.start()
        started.append(copy)
        return copy

    def ds(start, size):
        return pl.ds(start if isinstance(start, int) else pl.multiple_of(start, size), size)

    class Tensor:
        def __init__(self, full, shard_rows):
            self.full = full
            self.rows = shard_rows
            self.cols = full.shape[1]
            self.part = shard_rows // 2 // nx
            self.wide = self.cols // 2 // ny

        def box(self, h, xx, yy):
            row = h * (self.rows // 2) + xx * self.part
            return ds(row, self.part), ds((core * ny + yy) * self.wide, self.wide)

        def region(self, zs, h, xx, yy):
            row = zs * self.rows + h * (self.rows // 2) + xx * self.part
            return self.full.at[ds(row, self.part), ds((core * ny + yy) * self.wide, self.wide)]

        def first(self, src, d):
            return [
                send(src.at[self.box(h, x, y)], self.region(z, h, x, y), z_peer(d))
                for h in range(2)
            ]

        def second(self, zs, arrived):
            self.to_x, self.to_y = {}, {}
            out = ({}, {})
            for h in range(2):
                if arrived is not None:
                    arrived[h].wait_recv()
                mine = self.region(zs, h, x, y)
                for d in range(1, nx):
                    out[0][d, h] = send(mine, mine, x_peer(d))
                for d in range(1, ny):
                    out[1][d, h] = send(mine, mine, y_peer(d))
            return out

        def third(self, zs, out):
            later = []
            for d in range(1, nx):
                out[0][d, 0].wait_recv()
                got = self.region(zs, 0, shift(x, nx - d, nx), y)
                later += [send(got, got, y_peer(e)) for e in range(1, ny)]
            for d in range(1, ny):
                out[1][d, 1].wait_recv()
                got = self.region(zs, 1, x, shift(y, ny - d, ny))
                later += [send(got, got, x_peer(e)) for e in range(1, nx)]
            later += [out[0][d, 1] for d in range(1, nx)]
            later += [out[1][d, 0] for d in range(1, ny)]
            return later

        def fourth(self, zs, later):
            for copy in later:
                copy.wait_recv()
            half = self.full.at[ds(zs * self.rows, self.rows), ds(core * (self.cols // 2), self.cols // 2)]
            return send(half, half, mate)

    p_rows, h_rows = width // nz, dim // nz
    proj_t, head_t = Tensor(proj, p_rows), Tensor(head, h_rows)
    out_t = Tensor(gather, h_rows)

    loads = [
        pltpu.make_async_copy(proj_in, proj.at[ds(z * p_rows, p_rows)], local_sem.at[0]),
        pltpu.make_async_copy(rows_in, rows, local_sem.at[1]),
        pltpu.make_async_copy(head_in, head.at[ds(z * h_rows, h_rows)], local_sem.at[2]),
        pltpu.make_async_copy(gain_in, gains.at[z], local_sem.at[3]),
    ]
    for load in loads:
        load.start()
    barrier = pltpu.get_barrier_semaphore()
    for peer in peers:
        pl.semaphore_signal(barrier, inc=1, device_id=peer, device_id_type=pl.DeviceIdType.MESH)
    pl.semaphore_wait(barrier, len(peers))

    order = list(range(1, nz))
    order.sort(key=lambda d: min(d, nz - d))
    items = [(proj_t, d) for d in order] + [(head_t, d) for d in order]
    stage1 = {}
    for d in order:
        stage1[0, d] = proj_t.first(proj_in, d)
    gain_copies = [send(gain_in, gains.at[z], z_peer(d)) for d in order]
    for d in order:
        stage1[1, d] = head_t.first(head_in, d)
    for load in loads:
        load.wait()

    def project(zs, fresh):
        depth = ds(zs * p_rows, p_rows)

        @pl.loop(0, slots)
        def _(p):
            at = ds(p * pair_rows, pair_rows)
            part = jnp.dot(rows[at, depth], proj[depth, :], preferred_element_type=f32)
            acc[at, :] = part if fresh else acc[at, :] + part

    def score(zs, fresh):
        depth = ds(zs * h_rows, h_rows)

        @pl.loop(0, slots)
        def _(p):
            at = ds(p * pair_rows, pair_rows)
            part = jnp.dot(normed[at, depth], head[depth, :], preferred_element_type=f32)
            logits[at, :] = part if fresh else logits[at, :] + part

    def normalise():
        @pl.loop(0, slots * 2)
        def _(b):
            at = ds(b * frames, frames)
            kept = acc[at, :].astype(bf16)
            projected[at, :] = kept
            flat = kept.astype(f32)
            inv = lax.rsqrt(jnp.mean(flat * flat, axis=1, keepdims=True) + norm_eps)
            inverse[at, :] = inv
            for s in range(nz):
                cols = slice(s * h_rows, (s + 1) * h_rows)
                normed[at, cols] = (flat[:, cols] * inv * gains[s, 0:1, :]).astype(bf16)

    stage2, stage3, stage4 = {}, {}, {}
    for t in range(len(items) + 3):
        if t < len(items):
            tensor, d = items[t]
            which = 0 if tensor is proj_t else 1
            stage2[t] = tensor.second(shift(z, nz - d, nz), stage1[which, d])
        if t == 0:
            project(z, True)
        if 0 <= t - 1 < len(items):
            tensor, d = items[t - 1]
            stage3[t - 1] = tensor.third(shift(z, nz - d, nz), stage2[t - 1])
        if 0 <= t - 2 < len(items):
            tensor, d = items[t - 2]
            stage4[t - 2] = tensor.fourth(shift(z, nz - d, nz), stage3[t - 2])
        if 0 <= t - 3 < len(items):
            tensor, d = items[t - 3]
            stage4[t - 3].wait_recv()
            if tensor is proj_t:
                project(shift(z, nz - d, nz), False)
                if t - 3 == nz - 2:
                    for copy in gain_copies:
                        copy.wait_recv()
                    normalise()
                    score(z, True)
            else:
                score(shift(z, nz - d, nz), False)

    small[...] = jnp.zeros_like(small)

    @pl.loop(0, slots)
    def _(p):
        token = lax.broadcasted_iota(jnp.int32, (frames, vocab), 1)
        frame = lax.broadcasted_iota(jnp.int32, (frames, 1), 0)
        scores, sums, valids, sizes = [], [], [], []
        for b in range(2):
            at = ds(p * pair_rows + b * frames, frames)
            values = logits[at, :]
            highest = jnp.max(values, axis=1, keepdims=True)
            powers = jnp.exp(values - highest)
            total = jnp.sum(powers, axis=1, keepdims=True)
            picked = jnp.sum(jnp.where(token == codes[at, :], values, 0.0), axis=1, keepdims=True)
            logits[at, :] = powers
            length = lengths[p, b]
            valid = (frame < length).astype(f32)
            size = jnp.full((1, 1), length.astype(f32), f32)
            logp = picked - (highest + jnp.log(total))
            scores.append(jnp.sum(logp * valid, axis=0, keepdims=True) / size)
            sums.append(total)
            valids.append(valid)
            sizes.append(size)
        sign = jnp.where(labels[p] == 0, 1.0, -1.0).astype(f32)
        live = jnp.where(p < counts[0], 1.0, 0.0).astype(f32)
        margin = margin_scale * (sign * (scores[0] - scores[1]) - ratios[p])
        soft = jnp.maximum(-margin, 0.0) + jnp.log1p(jnp.exp(-jnp.abs(margin)))
        small[:, dim:] += jnp.broadcast_to(soft * live, (small.shape[0], small.shape[1] - dim))
        slope = -jax.nn.sigmoid(-margin) * live
        for b in range(2):
            at = ds(p * pair_rows + b * frames, frames)
            weight = (margin_scale if b == 0 else -margin_scale) * sign * slope / sizes[b]
            coeff = weight * valids[b]
            hot = jnp.where(token == codes[at, :], coeff, 0.0)
            dlogits[at, :] = (hot - (coeff / sums[b]) * logits[at, :]).astype(bf16)

    rx, cy = h_rows // 2 // nx, vocab // 2 // ny
    half_rows, half_cols = h_rows // 2, vocab // 2
    tile = min(512, half_cols)
    moves = list(range(1, nz)) + [0]
    one, two_x, two_y, three_x, three_y, z_copies = {}, {}, {}, {}, {}, {}

    def head_block(k):
        rows_at = ds(shift(z, moves[k], nz) * h_rows, h_rows)

        @pl.loop(0, vocab // tile)
        def _(j):
            cols = ds(j * tile, tile)
            term[k, :, cols] = lax.dot_general(
                normed[:, rows_at], dlogits[:, cols], (((0,), (0,)), ((), ())),
                preferred_element_type=f32,
            ).astype(bf16)

        one[k] = send(term.at[k, :, ds((1 - core) * half_cols, half_cols)], r1.at[k], mate)

    def sum_mates(k):
        one[k].wait_recv()
        mine = term[k, :, ds(core * half_cols, half_cols)].astype(f32)
        s1[k] = (mine + r1[k].astype(f32)).astype(bf16)
        for d in range(1, nx):
            two_x[k, d] = send(s1.at[k, ds(shift(x, d, nx) * rx, rx), :], ra0.at[k, d - 1], x_peer(d))
        for d in range(1, ny):
            two_y[k, d] = send(
                s1.at[k, ds(half_rows, half_rows), ds(shift(y, d, ny) * cy, cy)],
                ra1.at[k, d - 1], y_peer(d),
            )

    def sum_first(k):
        for d in range(1, nx):
            two_x[k, d].wait_recv()
        total = s1[k, ds(x * rx, rx), :].astype(f32)
        for d in range(1, nx):
            total = total + ra0[k, d - 1].astype(f32)
        s2a[k] = total.astype(bf16)
        for d in range(1, ny):
            three_y[k, d] = send(s2a.at[k, :, ds(shift(y, d, ny) * cy, cy)], rb0.at[k, d - 1], y_peer(d))
        for d in range(1, ny):
            two_y[k, d].wait_recv()
        total = s1[k, half_rows:, ds(y * cy, cy)].astype(f32)
        for d in range(1, ny):
            total = total + ra1[k, d - 1].astype(f32)
        s2b[k] = total.astype(bf16)
        for d in range(1, nx):
            three_x[k, d] = send(s2b.at[k, ds(shift(x, d, nx) * rx, rx), :], rb1.at[k, d - 1], x_peer(d))

    def sum_second(k):
        for d in range(1, ny):
            three_y[k, d].wait_recv()
        total = s2a[k, :, ds(y * cy, cy)].astype(f32)
        for d in range(1, ny):
            total = total + rb0[k, d - 1].astype(f32)
        s3[k, :rx, :] = total.astype(bf16)
        for d in range(1, nx):
            three_x[k, d].wait_recv()
        total = s2b[k, ds(x * rx, rx), :].astype(f32)
        for d in range(1, nx):
            total = total + rb1[k, d - 1].astype(f32)
        s3[k, rx:, :] = total.astype(bf16)
        if moves[k]:
            z_copies[moves[k]] = send(s3.at[k], r3.at[moves[k] - 1], z_peer(moves[k]))

    def gain_block(p):
        at = slice(p * pair_rows, (p + 1) * pair_rows)
        dnormed = lax.dot_general(
            dlogits[at, :], head[...], (((1,), (1,)), ((), ())), preferred_element_type=f32
        )
        part = jnp.sum(dnormed * (projected[at, :].astype(f32) * inverse[at, :]), axis=0, keepdims=True)
        small[:, :dim] += jnp.broadcast_to(part, (small.shape[0], dim))

    def share(buffer, value, mine, n, peer):
        buffer[mine] = value
        return [send(buffer.at[mine], buffer.at[mine], peer(d)) for d in range(1, n)]

    def collect(buffer, copies, n):
        for copy in copies:
            copy.wait_recv()
        total = buffer[0]
        for i in range(1, n):
            total = total + buffer[i]
        return total

    small_copies = None
    for t in range(max(nz, slots) + 4):
        if t < nz:
            head_block(t)
        if 0 <= t - 1 < nz:
            sum_mates(t - 1)
        if 0 <= t - 2 < nz:
            sum_first(t - 2)
        if 0 <= t - 3 < nz:
            sum_second(t - 3)
        if 0 <= t - 1 < slots:
            gain_block(t - 1)
        if t == slots:
            small_copies = share(sum_c, small[...], core, 2, lambda d: mate)
        if t == slots + 1:
            value = collect(sum_c, small_copies, 2)
            small_copies = share(sum_x, value, x, nx, x_peer)
        if t == slots + 2:
            value = collect(sum_x, small_copies, nx)
            small_copies = share(sum_y, value, y, ny, y_peer)
        if t == slots + 3:
            value = collect(sum_y, small_copies, ny)
            small_copies = share(sum_z, value, z, nz, z_peer)

    total = s3[nz - 1].astype(f32)
    for d in range(1, nz):
        z_copies[d].wait_recv()
        total = total + r3[d - 1].astype(f32)
    for h in range(2):
        gather[out_t.box(h, x, y)] = total[h * rx : (h + 1) * rx, :].astype(bf16)
    last = out_t.second(0, None)
    value = collect(sum_z, small_copies, nz)
    small[...] = value
    loss_out[...] = value[:, dim:] / pair_total
    gain_out[...] = small[:, ds(z * h_rows, h_rows)]
    last = out_t.fourth(0, out_t.third(0, last))
    mine = ds(core * half_cols, half_cols)
    grad_out[:, mine] = gather[:, mine].astype(f32)
    last.wait_recv()
    other = ds((1 - core) * half_cols, half_cols)
    grad_out[:, other] = gather[:, other].astype(f32)
    for copy in started:
        copy.wait_send()


def on_device(
    thinker_rows, codec_ids, block_lengths, chosen_label, ref_logratio, pair_count,
    proj_weight, norm_gain, head_weight,
):
    slots, frames, width = thinker_rows.shape[2], thinker_rows.shape[4], thinker_rows.shape[5]
    dim, vocab = proj_weight.shape[1], head_weight.shape[1]
    wide, nz = lax.axis_size("wide"), lax.axis_size("narrow")
    ny, nx = plane_of(wide)
    count = slots * 2 * frames
    hold = (slots + 1) // 2
    h_rows = dim // nz
    rx, cy = h_rows // 2 // nx, vocab // 2 // ny
    half = vocab // 2
    n = copy_count(nx, ny, nz)
    vmem, smem = pl.BlockSpec(memory_space=pltpu.VMEM), pl.BlockSpec(memory_space=pltpu.SMEM)
    hbm = pl.BlockSpec(memory_space=pl.ANY)
    line = (8, dim + 128)
    scratch = [
        pltpu.VMEM((count, width), bf16),
        pltpu.VMEM((width, dim), bf16),
        pltpu.VMEM((dim, vocab), bf16),
        pltpu.VMEM((nz, 8, h_rows), f32),
        pltpu.VMEM((count, dim), f32),
        pltpu.VMEM((count, dim), bf16),
        pltpu.VMEM((count, 1), f32),
        pltpu.VMEM((count, dim), bf16),
        pltpu.VMEM((count, vocab), f32),
        pltpu.VMEM((count, vocab), bf16),
        pltpu.VMEM((nz, h_rows, vocab), bf16),
        pltpu.VMEM((nz, h_rows, half), bf16),
        pltpu.VMEM((nz, h_rows, half), bf16),
        pltpu.VMEM((nz, nx - 1, rx, half), bf16),
        pltpu.VMEM((nz, ny - 1, h_rows // 2, cy), bf16),
        pltpu.VMEM((nz, rx, half), bf16),
        pltpu.VMEM((nz, h_rows // 2, cy), bf16),
        pltpu.VMEM((nz, ny - 1, rx, cy), bf16),
        pltpu.VMEM((nz, nx - 1, rx, cy), bf16),
        pltpu.VMEM((nz, 2 * rx, cy), bf16),
        pltpu.VMEM((nz - 1, 2 * rx, cy), bf16),
        pltpu.VMEM((h_rows, vocab), bf16),
        pltpu.VMEM(line, f32),
        pltpu.VMEM((2,) + line, f32),
        pltpu.VMEM((nx,) + line, f32),
        pltpu.VMEM((ny,) + line, f32),
        pltpu.VMEM((nz,) + line, f32),
        pltpu.SemaphoreType.DMA((4,)),
        pltpu.SemaphoreType.DMA((n,)),
        pltpu.SemaphoreType.DMA((n,)),
    ]
    loss, grad_head, grad_gain = pl.pallas_call(
        functools.partial(
            kernel, ny, nx, nz, slots, frames, width, dim, vocab, float(wide * nz * hold)
        ),
        out_shape=[
            jax.ShapeDtypeStruct((8, 128), f32),
            jax.ShapeDtypeStruct((h_rows, vocab), f32),
            jax.ShapeDtypeStruct((8, h_rows), f32),
        ],
        in_specs=[smem, smem, smem, smem, hbm, vmem, hbm, hbm, hbm],
        out_specs=[vmem, vmem, vmem],
        scratch_shapes=scratch,
        compiler_params=pltpu.CompilerParams(
            collective_id=0, has_side_effects=True, vmem_limit_bytes=58 * 1024 * 1024
        ),
        cost_estimate=pl.CostEstimate(
            flops=8 * count * width * dim, bytes_accessed=count * width * 8, transcendentals=count * vocab
        ),
    )(
        block_lengths[0, 0],
        chosen_label[0, 0],
        pair_count[0],
        ref_logratio[0, 0],
        thinker_rows.reshape(count, width),
        codec_ids.reshape(count, 1),
        proj_weight,
        jnp.broadcast_to(norm_gain.astype(f32)[None, :], (8, h_rows)),
        head_weight,
    )
    return loss[0, 0], grad_head, grad_gain[0]


def solution(mesh):
    in_specs = (
        P("wide", "narrow", None, None, None, None),
        P("wide", "narrow", None, None, None),
        P("wide", "narrow", None, None),
        P("wide", "narrow", None),
        P("wide", "narrow", None),
        P("wide", "narrow"),
        P("narrow", None),
        P("narrow"),
        P("narrow", None),
    )
    out_specs = (P(), P("narrow", None), P("narrow"))
    return jax.shard_map(
        on_device, mesh=mesh, in_specs=in_specs, out_specs=out_specs, check_vma=False
    )
```

```python
import functools

import jax
import jax.numpy as jnp
from jax import lax
from jax.experimental import pallas as pl
from jax.experimental.pallas import tpu as pltpu
from jax.sharding import PartitionSpec as P

norm_eps = 1e-06
margin_scale = 2.0
f32 = jnp.float32
bf16 = jnp.bfloat16


def plane_of(wide):
    chips = wide // 2
    rows = 1
    while (rows * 2) * (rows * 2) <= chips:
        rows *= 2
    return rows, chips // rows


def spread_count(nx, ny):
    return 2 * (nx - 1) + 2 * (ny - 1) + 2 * (nx - 1) * (ny - 1) + 1


def copy_count(nx, ny, nz):
    weights = 2 * (nz - 1) * spread_count(nx, ny) + (nz - 1)
    sums = nz * (1 + 2 * (nx - 1) + 2 * (ny - 1)) + (nz - 1)
    small = 1 + (nx - 1) + (ny - 1) + (nz - 1)
    return weights + sums + spread_count(nx, ny) + small


def kernel(
    ny, nx, nz, slots, frames, width, dim, vocab, pair_total,
    labels, counts, ratios, lengths, codes, gain_in,
    rows_in, proj_in, head_in,
    loss_out, grad_out, gain_out,
    rows, proj, head, gains, acc, projected, inverse, normed, normed_t, logits, dlogits,
    term, r1, s1, ra0, ra1, s2a, s2b, rb0, rb1, s3, r3, gather,
    small, sum_c, sum_x, sum_y, sum_z,
    local_sem, send_sem, recv_sem, line_send, line_recv,
):
    w = lax.axis_index("wide")
    z = lax.axis_index("narrow")
    core = lax.rem(w, 2)
    chip = lax.div(w, 2)
    x = lax.rem(chip, nx)
    y = lax.div(chip, nx)
    pair_rows = 2 * frames
    total_rows = slots * pair_rows

    def wide_at(yy, xx, cc):
        return (yy * nx + xx) * 2 + cc

    def shift(i, d, n):
        return lax.rem(i + d, n)

    def x_peer(d):
        return {"wide": wide_at(y, shift(x, d, nx), core), "narrow": z}

    def y_peer(d):
        return {"wide": wide_at(shift(y, d, ny), x, core), "narrow": z}

    def z_peer(d):
        return {"wide": w, "narrow": shift(z, d, nz)}

    mate = {"wide": wide_at(y, x, 1 - core), "narrow": z}
    peers = [mate]
    peers += [x_peer(d) for d in range(1, nx)]
    peers += [y_peer(d) for d in range(1, ny)]
    peers += [z_peer(d) for d in range(1, nz)]

    started = []

    def send(src, dst, device):
        at = len(started)
        copy = pltpu.make_async_remote_copy(
            src_ref=src,
            dst_ref=dst,
            send_sem=send_sem.at[at],
            recv_sem=recv_sem.at[at],
            device_id=device,
            device_id_type=pl.DeviceIdType.MESH,
        )
        copy.start()
        started.append(copy)
        return copy

    def ds(start, size):
        return pl.ds(start if isinstance(start, int) else pl.multiple_of(start, size), size)

    class Tensor:
        def __init__(self, full, shard_rows):
            self.full = full
            self.rows = shard_rows
            self.cols = full.shape[1]
            self.part = shard_rows // 2 // nx
            self.wide = self.cols // 2 // ny

        def box(self, h, xx, yy):
            row = h * (self.rows // 2) + xx * self.part
            return ds(row, self.part), ds((core * ny + yy) * self.wide, self.wide)

        def region(self, zs, h, xx, yy):
            row = zs * self.rows + h * (self.rows // 2) + xx * self.part
            return self.full.at[ds(row, self.part), ds((core * ny + yy) * self.wide, self.wide)]

        def line(self, src, zs, h, send_at, target):
            which = 0 if self is proj_t else 1
            here = self.region(zs, h, x, y)
            return pltpu.make_async_remote_copy(
                src_ref=here if src is None else src.at[self.box(h, x, y)],
                dst_ref=here,
                send_sem=line_send.at[which, h, send_at],
                recv_sem=line_recv.at[which, h, zs],
                device_id={"wide": w, "narrow": target},
                device_id_type=pl.DeviceIdType.MESH,
            )

        def begin(self, src):
            for h in range(2):
                @pl.when(z + 1 < nz)
                def _():
                    self.line(src, z, h, z, z + 1).start()

                @pl.when(z > 0)
                def _():
                    self.line(src, z, h, nz, z - 1).start()

        def arrive(self, zs, h):
            self.line(None, zs, h, zs, lax.rem(z + 1, nz)).wait_recv()

            @pl.when((zs < z) & (z + 1 < nz))
            def _():
                self.line(None, zs, h, zs, z + 1).start()

            @pl.when((zs > z) & (z > 0))
            def _():
                self.line(None, zs, h, zs, z - 1).start()

        def finish(self, src, sources):
            for h in range(2):
                @pl.when(z + 1 < nz)
                def _():
                    self.line(src, z, h, z, z + 1).wait_send()

                @pl.when(z > 0)
                def _():
                    self.line(src, z, h, nz, z - 1).wait_send()

                for zs in sources:
                    @pl.when((zs < z) & (z + 1 < nz))
                    def _():
                        self.line(None, zs, h, zs, z + 1).wait_send()

                    @pl.when((zs > z) & (z > 0))
                    def _():
                        self.line(None, zs, h, zs, z - 1).wait_send()

        def second(self, zs, arrives):
            out = ({}, {})
            for h in range(2):
                if arrives:
                    self.arrive(zs, h)
                mine = self.region(zs, h, x, y)
                for d in range(1, nx):
                    out[0][d, h] = send(mine, mine, x_peer(d))
                for d in range(1, ny):
                    out[1][d, h] = send(mine, mine, y_peer(d))
            return out

        def third(self, zs, out):
            later = []
            for d in range(1, nx):
                out[0][d, 0].wait_recv()
                got = self.region(zs, 0, shift(x, nx - d, nx), y)
                later += [send(got, got, y_peer(e)) for e in range(1, ny)]
            for d in range(1, ny):
                out[1][d, 1].wait_recv()
                got = self.region(zs, 1, x, shift(y, ny - d, ny))
                later += [send(got, got, x_peer(e)) for e in range(1, nx)]
            later += [out[0][d, 1] for d in range(1, nx)]
            later += [out[1][d, 0] for d in range(1, ny)]
            return later

        def fourth(self, zs, later):
            for copy in later:
                copy.wait_recv()
            half = self.full.at[ds(zs * self.rows, self.rows), ds(core * (self.cols // 2), self.cols // 2)]
            return send(half, half, mate)

    p_rows, h_rows = width // nz, dim // nz
    proj_t, head_t = Tensor(proj, p_rows), Tensor(head, h_rows)
    out_t = Tensor(gather, h_rows)

    loads = [
        pltpu.make_async_copy(proj_in, proj.at[ds(z * p_rows, p_rows)], local_sem.at[0]),
        pltpu.make_async_copy(rows_in, rows, local_sem.at[1]),
        pltpu.make_async_copy(head_in, head.at[ds(z * h_rows, h_rows)], local_sem.at[2]),
    ]
    for load in loads:
        load.start()
    barrier = pltpu.get_barrier_semaphore()
    for peer in peers:
        pl.semaphore_signal(barrier, inc=1, device_id=peer, device_id_type=pl.DeviceIdType.MESH)
    pl.semaphore_wait(barrier, len(peers))

    proj_t.begin(proj_in)
    gains[z] = jnp.broadcast_to(gain_in[...].astype(f32).reshape(1, h_rows), (8, h_rows))
    gain_copies = [send(gains.at[z], gains.at[z], z_peer(d)) for d in range(1, nz)]
    near = jnp.minimum(z, nz - 1 - z)
    sources = []
    for j in range(nz - 1):
        both = j < 2 * near
        dist = jnp.where(both, j // 2 + 1, j - near + 1)
        down = jnp.where(both, j % 2 == 0, z > nz - 1 - z)
        sources.append(jnp.where(down, z - dist, z + dist))
    items = [(proj_t, zs) for zs in sources] + [(head_t, zs) for zs in sources]
    for load in loads:
        load.wait()

    def project(zs, fresh):
        depth = ds(zs * p_rows, p_rows)

        @pl.loop(0, slots)
        def _(p):
            at = ds(p * pair_rows, pair_rows)
            part = jnp.dot(rows[at, depth], proj[depth, :], preferred_element_type=f32)
            acc[at, :] = part if fresh else acc[at, :] + part

    def score(zs, fresh):
        depth = ds(zs * h_rows, h_rows)

        @pl.loop(0, slots)
        def _(p):
            at = ds(p * pair_rows, pair_rows)
            part = jnp.dot(normed[at, depth], head[depth, :], preferred_element_type=f32)
            logits[at, :] = part if fresh else logits[at, :] + part

    def normalise():
        @pl.loop(0, slots * 2)
        def _(b):
            at = ds(b * frames, frames)
            kept = acc[at, :].astype(bf16)
            projected[at, :] = kept
            flat = kept.astype(f32)
            inv = lax.rsqrt(jnp.mean(flat * flat, axis=1, keepdims=True) + norm_eps)
            inverse[at, :] = inv
            for s in range(nz):
                cols = slice(s * h_rows, (s + 1) * h_rows)
                part = flat[:, cols] * inv * gains[s, 0:1, :]
                normed[at, cols] = part.astype(bf16)
                normed_t[cols, at] = jnp.transpose(part).astype(bf16)

    stage2, stage3, stage4 = {}, {}, {}
    for t in range(len(items) + 3):
        if t < len(items):
            tensor, zs = items[t]
            stage2[t] = tensor.second(zs, True)
        if t == 0:
            head_t.begin(head_in)
            project(z, True)
        if 0 <= t - 1 < len(items):
            tensor, zs = items[t - 1]
            stage3[t - 1] = tensor.third(zs, stage2[t - 1])
        if 0 <= t - 2 < len(items):
            tensor, zs = items[t - 2]
            stage4[t - 2] = tensor.fourth(zs, stage3[t - 2])
        if 0 <= t - 3 < len(items):
            tensor, zs = items[t - 3]
            stage4[t - 3].wait_recv()
            if tensor is proj_t:
                project(zs, False)
                if t - 3 == nz - 2:
                    for copy in gain_copies:
                        copy.wait_recv()
                    normalise()
                    score(z, True)
            else:
                score(zs, False)

    small[...] = jnp.zeros_like(small)

    @pl.loop(0, slots)
    def _(p):
        token = lax.broadcasted_iota(jnp.int32, (frames, vocab), 1)
        frame = lax.broadcasted_iota(jnp.int32, (frames, 1), 0)
        scores, sums, valids, sizes, columns = [], [], [], [], []
        for b in range(2):
            at = ds(p * pair_rows + b * frames, frames)
            values = logits[at, :]
            highest = jnp.max(values, axis=1, keepdims=True)
            powers = jnp.exp(values - highest)
            total = jnp.sum(powers, axis=1, keepdims=True)
            line = codes[0, 0, p, b : b + 1, :].astype(f32)
            column = jnp.transpose(jnp.broadcast_to(line, (frames, frames)))[:, 0:1].astype(jnp.int32)
            picked = jnp.sum(jnp.where(token == column, values, 0.0), axis=1, keepdims=True)
            logits[at, :] = powers
            held = lengths[0, 0, b : b + 1, :].astype(f32)
            slot = lax.broadcasted_iota(jnp.int32, (1, slots), 1)
            size = jnp.sum(jnp.where(slot == p, held, 0.0), axis=1, keepdims=True)
            valid = (frame.astype(f32) < size).astype(f32)
            logp = picked - (highest + jnp.log(total))
            scores.append(jnp.sum(logp * valid, axis=0, keepdims=True) / size)
            sums.append(total)
            columns.append(column)
            valids.append(valid)
            sizes.append(size)
        sign = jnp.where(labels[p] == 0, 1.0, -1.0).astype(f32)
        live = jnp.where(p < counts[0], 1.0, 0.0).astype(f32)
        margin = margin_scale * (sign * (scores[0] - scores[1]) - ratios[p])
        soft = jnp.maximum(-margin, 0.0) + jnp.log1p(jnp.exp(-jnp.abs(margin)))
        small[:, dim:] += jnp.broadcast_to(soft * live, (small.shape[0], small.shape[1] - dim))
        slope = -jax.nn.sigmoid(-margin) * live
        for b in range(2):
            at = ds(p * pair_rows + b * frames, frames)
            weight = (margin_scale if b == 0 else -margin_scale) * sign * slope / sizes[b]
            coeff = weight * valids[b]
            hot = jnp.where(token == columns[b], coeff, 0.0)
            dlogits[at, :] = (hot - (coeff / sums[b]) * logits[at, :]).astype(bf16)

    rx, cy = h_rows // 2 // nx, vocab // 2 // ny
    half_rows, half_cols = h_rows // 2, vocab // 2
    tile = min(512, half_cols)
    moves = list(range(1, nz)) + [0]
    one, two_x, two_y, three_x, three_y, z_copies = {}, {}, {}, {}, {}, {}

    def head_block(k):
        rows_at = ds(shift(z, moves[k], nz) * h_rows, h_rows)

        @pl.loop(0, vocab // tile)
        def _(j):
            cols = ds(j * tile, tile)
            term[k, :, cols] = jnp.dot(
                normed_t[rows_at, :], dlogits[:, cols], preferred_element_type=f32
            ).astype(bf16)

        one[k] = send(term.at[k, :, ds((1 - core) * half_cols, half_cols)], r1.at[k], mate)

    def sum_mates(k):
        one[k].wait_recv()
        mine = term[k, :, ds(core * half_cols, half_cols)].astype(f32)
        s1[k] = (mine + r1[k].astype(f32)).astype(bf16)
        for d in range(1, nx):
            two_x[k, d] = send(s1.at[k, ds(shift(x, d, nx) * rx, rx), :], ra0.at[k, d - 1], x_peer(d))
        for d in range(1, ny):
            two_y[k, d] = send(
                s1.at[k, ds(half_rows, half_rows), ds(shift(y, d, ny) * cy, cy)],
                ra1.at[k, d - 1], y_peer(d),
            )

    def sum_first(k):
        for d in range(1, nx):
            two_x[k, d].wait_recv()
        total = s1[k, ds(x * rx, rx), :].astype(f32)
        for d in range(1, nx):
            total = total + ra0[k, d - 1].astype(f32)
        s2a[k] = total.astype(bf16)
        for d in range(1, ny):
            three_y[k, d] = send(s2a.at[k, :, ds(shift(y, d, ny) * cy, cy)], rb0.at[k, d - 1], y_peer(d))
        for d in range(1, ny):
            two_y[k, d].wait_recv()
        total = s1[k, half_rows:, ds(y * cy, cy)].astype(f32)
        for d in range(1, ny):
            total = total + ra1[k, d - 1].astype(f32)
        s2b[k] = total.astype(bf16)
        for d in range(1, nx):
            three_x[k, d] = send(s2b.at[k, ds(shift(x, d, nx) * rx, rx), :], rb1.at[k, d - 1], x_peer(d))

    def sum_second(k):
        for d in range(1, ny):
            three_y[k, d].wait_recv()
        total = s2a[k, :, ds(y * cy, cy)].astype(f32)
        for d in range(1, ny):
            total = total + rb0[k, d - 1].astype(f32)
        s3[k, :rx, :] = total.astype(bf16)
        for d in range(1, nx):
            three_x[k, d].wait_recv()
        total = s2b[k, ds(x * rx, rx), :].astype(f32)
        for d in range(1, nx):
            total = total + rb1[k, d - 1].astype(f32)
        s3[k, rx:, :] = total.astype(bf16)
        if moves[k]:
            z_copies[moves[k]] = send(s3.at[k], r3.at[moves[k] - 1], z_peer(moves[k]))

    def gain_block(p):
        at = slice(p * pair_rows, (p + 1) * pair_rows)
        dnormed = lax.dot_general(
            dlogits[at, :], head[...], (((1,), (1,)), ((), ())), preferred_element_type=f32
        )
        part = jnp.sum(dnormed * (projected[at, :].astype(f32) * inverse[at, :]), axis=0, keepdims=True)
        small[:, :dim] += jnp.broadcast_to(part, (small.shape[0], dim))

    def share(buffer, value, mine, n, peer):
        buffer[mine] = value
        return [send(buffer.at[mine], buffer.at[mine], peer(d)) for d in range(1, n)]

    def collect(buffer, copies, n):
        for copy in copies:
            copy.wait_recv()
        total = buffer[0]
        for i in range(1, n):
            total = total + buffer[i]
        return total

    small_copies = None
    for t in range(max(nz, slots) + 3):
        if t < nz:
            head_block(t)
        if 0 <= t - 1 < nz:
            sum_mates(t - 1)
        if 0 <= t - 2 < nz:
            sum_first(t - 2)
        if 0 <= t - 3 < nz:
            sum_second(t - 3)
        if 0 <= t - 1 < slots:
            gain_block(t - 1)
        if t == slots:
            small_copies = share(sum_c, small[...], core, 2, lambda d: mate)
        if t == slots + 1:
            value = collect(sum_c, small_copies, 2)
            small_copies = share(sum_x, value, x, nx, x_peer)
        if t == slots + 2:
            value = collect(sum_x, small_copies, nx)
            small_copies = share(sum_y, value, y, ny, y_peer)

    total = s3[nz - 1].astype(f32)
    for d in range(1, nz):
        z_copies[d].wait_recv()
        total = total + r3[d - 1].astype(f32)
    for h in range(2):
        gather[out_t.box(h, x, y)] = total[h * rx : (h + 1) * rx, :].astype(bf16)
    last = out_t.second(0, False)
    value = collect(sum_y, small_copies, ny)
    small_copies = share(sum_z, value, z, nz, z_peer)
    last = out_t.fourth(0, out_t.third(0, last))
    mine = ds(core * half_cols, half_cols)
    stores = [pltpu.make_async_copy(gather.at[:, mine], grad_out.at[:, mine], local_sem.at[0])]
    stores[0].start()
    value = collect(sum_z, small_copies, nz)
    small[...] = value
    loss_out[...] = value[0:1, dim : dim + 1] / pair_total
    gain_out[...] = small[0:1, ds(z * h_rows, h_rows)]
    last.wait_recv()
    other = ds((1 - core) * half_cols, half_cols)
    stores.append(pltpu.make_async_copy(gather.at[:, other], grad_out.at[:, other], local_sem.at[1]))
    stores[1].start()
    for store in stores:
        store.wait()
    for copy in started:
        copy.wait_send()
    proj_t.finish(proj_in, sources)
    head_t.finish(head_in, sources)


def on_device(
    thinker_rows, codec_ids, block_lengths, chosen_label, ref_logratio, pair_count,
    proj_weight, norm_gain, head_weight,
):
    slots, frames, width = thinker_rows.shape[2], thinker_rows.shape[4], thinker_rows.shape[5]
    dim, vocab = proj_weight.shape[1], head_weight.shape[1]
    wide, nz = lax.axis_size("wide"), lax.axis_size("narrow")
    ny, nx = plane_of(wide)
    count = slots * 2 * frames
    hold = (slots + 1) // 2
    h_rows = dim // nz
    rx, cy = h_rows // 2 // nx, vocab // 2 // ny
    half = vocab // 2
    n = copy_count(nx, ny, nz)
    vmem, smem = pl.BlockSpec(memory_space=pltpu.VMEM), pl.BlockSpec(memory_space=pltpu.SMEM)
    hbm = pl.BlockSpec(memory_space=pl.ANY)
    line = (8, dim + 128)
    scratch = [
        pltpu.VMEM((count, width), bf16),
        pltpu.VMEM((width, dim), bf16),
        pltpu.VMEM((dim, vocab), bf16),
        pltpu.VMEM((nz, 8, h_rows), f32),
        pltpu.VMEM((count, dim), f32),
        pltpu.VMEM((count, dim), bf16),
        pltpu.VMEM((count, 1), f32),
        pltpu.VMEM((count, dim), bf16),
        pltpu.VMEM((dim, count), bf16),
        pltpu.VMEM((count, vocab), f32),
        pltpu.VMEM((count, vocab), bf16),
        pltpu.VMEM((nz, h_rows, vocab), bf16),
        pltpu.VMEM((nz, h_rows, half), bf16),
        pltpu.VMEM((nz, h_rows, half), bf16),
        pltpu.VMEM((nz, nx - 1, rx, half), bf16),
        pltpu.VMEM((nz, ny - 1, h_rows // 2, cy), bf16),
        pltpu.VMEM((nz, rx, half), bf16),
        pltpu.VMEM((nz, h_rows // 2, cy), bf16),
        pltpu.VMEM((nz, ny - 1, rx, cy), bf16),
        pltpu.VMEM((nz, nx - 1, rx, cy), bf16),
        pltpu.VMEM((nz, 2 * rx, cy), bf16),
        pltpu.VMEM((nz - 1, 2 * rx, cy), bf16),
        pltpu.VMEM((h_rows, vocab), bf16),
        pltpu.VMEM(line, f32),
        pltpu.VMEM((2,) + line, f32),
        pltpu.VMEM((nx,) + line, f32),
        pltpu.VMEM((ny,) + line, f32),
        pltpu.VMEM((nz,) + line, f32),
        pltpu.SemaphoreType.DMA((4,)),
        pltpu.SemaphoreType.DMA((n,)),
        pltpu.SemaphoreType.DMA((n,)),
        pltpu.SemaphoreType.DMA((2, 2, nz + 1)),
        pltpu.SemaphoreType.DMA((2, 2, nz)),
    ]
    loss, grad_head, grad_gain = pl.pallas_call(
        functools.partial(
            kernel, ny, nx, nz, slots, frames, width, dim, vocab, float(wide * nz * hold)
        ),
        out_shape=[
            jax.ShapeDtypeStruct((1, 1), f32),
            jax.ShapeDtypeStruct((h_rows, vocab), bf16),
            jax.ShapeDtypeStruct((1, h_rows), f32),
        ],
        in_specs=[smem, smem, smem, vmem, vmem, vmem, hbm, hbm, hbm],
        out_specs=[vmem, hbm, vmem],
        scratch_shapes=scratch,
        compiler_params=pltpu.CompilerParams(
            collective_id=0, has_side_effects=True, vmem_limit_bytes=58 * 1024 * 1024
        ),
        cost_estimate=pl.CostEstimate(
            flops=8 * count * width * dim, bytes_accessed=count * width * 8, transcendentals=count * vocab
        ),
    )(
        chosen_label[0, 0],
        pair_count[0],
        ref_logratio[0, 0],
        jnp.swapaxes(block_lengths, 2, 3),
        codec_ids,
        norm_gain,
        thinker_rows.reshape(count, width),
        proj_weight,
        head_weight,
    )
    return loss[0, 0], grad_head.astype(f32), grad_gain[0]


def solution(mesh):
    in_specs = (
        P("wide", "narrow", None, None, None, None),
        P("wide", "narrow", None, None, None),
        P("wide", "narrow", None, None),
        P("wide", "narrow", None),
        P("wide", "narrow", None),
        P("wide", "narrow"),
        P("narrow", None),
        P("narrow"),
        P("narrow", None),
    )
    out_specs = (P(), P("narrow", None), P("narrow"))
    return jax.shard_map(
        on_device, mesh=mesh, in_specs=in_specs, out_specs=out_specs, check_vma=False
    )
```

```python
import functools

import jax
import jax.numpy as jnp
from jax import lax
from jax.experimental import pallas as pl
from jax.experimental.pallas import tpu as pltpu
from jax.sharding import PartitionSpec as P

norm_eps = 1e-06
margin_scale = 2.0
halves = 2
f32 = jnp.float32
bf16 = jnp.bfloat16


def plane_of(wide):
    chips = wide // 2
    rows = 1
    while (rows * 2) * (rows * 2) <= chips:
        rows *= 2
    return rows, chips // rows


def spread_count(nx, ny):
    return 2 * (nx - 1) + 2 * (ny - 1) + 2 * (nx - 1) * (ny - 1) + 1


def copy_count(nx, ny, nz):
    weights = 3 * (nz - 1) * spread_count(nx, ny) + (nz - 1)
    sums = halves * (nz * (1 + 2 * (nx - 1) + 2 * (ny - 1)) + (nz - 1))
    small = (nz - 1) + (2 * nx * ny - 1)
    return weights + sums + halves * spread_count(nx, ny) + small


def kernel(
    ny, nx, nz, slots, frames, width, dim, vocab, pair_total,
    labels, counts, ratios, lengths, codes, gain_in,
    rows_in, proj_in, head_in,
    loss_out, grad_out, gain_out,
    rows, proj, head, gains, acc, projected, inverse, normed, normed_t, logits, dlogits,
    term, r1, s1, ra0, ra1, s2a, s2b, rb0, rb1, s3, r3, gather,
    small, sum_z, sum_w,
    local_sem, send_sem, recv_sem, line_send, line_recv,
):
    w = lax.axis_index("wide")
    z = lax.axis_index("narrow")
    core = lax.rem(w, 2)
    chip = lax.div(w, 2)
    x = lax.rem(chip, nx)
    y = lax.div(chip, nx)
    pair_rows = 2 * frames
    total_rows = slots * pair_rows

    def wide_at(yy, xx, cc):
        return (yy * nx + xx) * 2 + cc

    def shift(i, d, n):
        return lax.rem(i + d, n)

    def x_peer(d):
        return {"wide": wide_at(y, shift(x, d, nx), core), "narrow": z}

    def y_peer(d):
        return {"wide": wide_at(shift(y, d, ny), x, core), "narrow": z}

    def z_peer(d):
        return {"wide": w, "narrow": shift(z, d, nz)}

    wide = ny * nx * 2
    mate = {"wide": wide_at(y, x, 1 - core), "narrow": z}

    def w_peer(d):
        return {"wide": shift(w, d, wide), "narrow": z}

    peers = [w_peer(d) for d in range(1, wide)]
    peers += [z_peer(d) for d in range(1, nz)]

    started = []

    def send(src, dst, device):
        at = len(started)
        copy = pltpu.make_async_remote_copy(
            src_ref=src,
            dst_ref=dst,
            send_sem=send_sem.at[at],
            recv_sem=recv_sem.at[at],
            device_id=device,
            device_id_type=pl.DeviceIdType.MESH,
        )
        copy.start()
        started.append(copy)
        return copy

    def ds(start, size):
        return pl.ds(start if isinstance(start, int) else pl.multiple_of(start, size), size)

    class Tensor:
        def __init__(self, full, shard_rows, base, cols, index):
            self.full = full
            self.rows = shard_rows
            self.base = base
            self.cols = cols
            self.index = index
            self.part = shard_rows // 2 // nx
            self.wide = cols // 2 // ny

        def columns(self, yy):
            return ds(self.base + (core * ny + yy) * self.wide, self.wide)

        def box(self, h, xx, yy):
            return ds(h * (self.rows // 2) + xx * self.part, self.part), self.columns(yy)

        def region(self, zs, h, xx, yy):
            row = zs * self.rows + h * (self.rows // 2) + xx * self.part
            return self.full.at[ds(row, self.part), self.columns(yy)]

        def line(self, src, zs, h, send_at, target):
            which = self.index
            here = self.region(zs, h, x, y)
            return pltpu.make_async_remote_copy(
                src_ref=here if src is None else src.at[self.box(h, x, y)],
                dst_ref=here,
                send_sem=line_send.at[which, h, send_at],
                recv_sem=line_recv.at[which, h, zs],
                device_id={"wide": w, "narrow": target},
                device_id_type=pl.DeviceIdType.MESH,
            )

        def begin(self, src):
            for h in range(2):
                @pl.when(z + 1 < nz)
                def _():
                    self.line(src, z, h, z, z + 1).start()

                @pl.when(z > 0)
                def _():
                    self.line(src, z, h, nz, z - 1).start()

        def arrive(self, zs, h):
            self.line(None, zs, h, zs, lax.rem(z + 1, nz)).wait_recv()

            @pl.when((zs < z) & (z + 1 < nz))
            def _():
                self.line(None, zs, h, zs, z + 1).start()

            @pl.when((zs > z) & (z > 0))
            def _():
                self.line(None, zs, h, zs, z - 1).start()

        def finish(self, src, sources):
            for h in range(2):
                @pl.when(z + 1 < nz)
                def _():
                    self.line(src, z, h, z, z + 1).wait_send()

                @pl.when(z > 0)
                def _():
                    self.line(src, z, h, nz, z - 1).wait_send()

                for zs in sources:
                    @pl.when((zs < z) & (z + 1 < nz))
                    def _():
                        self.line(None, zs, h, zs, z + 1).wait_send()

                    @pl.when((zs > z) & (z > 0))
                    def _():
                        self.line(None, zs, h, zs, z - 1).wait_send()

        def second(self, zs, arrives):
            out = ({}, {})
            for h in range(2):
                if arrives:
                    self.arrive(zs, h)
                mine = self.region(zs, h, x, y)
                for d in range(1, nx):
                    out[0][d, h] = send(mine, mine, x_peer(d))
                for d in range(1, ny):
                    out[1][d, h] = send(mine, mine, y_peer(d))
            return out

        def third(self, zs, out):
            later = []
            for d in range(1, nx):
                out[0][d, 0].wait_recv()
                got = self.region(zs, 0, shift(x, nx - d, nx), y)
                later += [send(got, got, y_peer(e)) for e in range(1, ny)]
            for d in range(1, ny):
                out[1][d, 1].wait_recv()
                got = self.region(zs, 1, x, shift(y, ny - d, ny))
                later += [send(got, got, x_peer(e)) for e in range(1, nx)]
            later += [out[0][d, 1] for d in range(1, nx)]
            later += [out[1][d, 0] for d in range(1, ny)]
            return later

        def fourth(self, zs, later):
            for copy in later:
                copy.wait_recv()
            half = self.full.at[ds(zs * self.rows, self.rows), ds(self.base + core * (self.cols // 2), self.cols // 2)]
            return send(half, half, mate)

    p_rows, h_rows = width // nz, dim // nz
    piece = vocab // halves
    proj_t = Tensor(proj, p_rows, 0, dim, 0)
    head_t = [Tensor(head, h_rows, q * piece, piece, 1 + q) for q in range(halves)]
    out_t = [Tensor(gather, h_rows, q * piece, piece, 0) for q in range(halves)]

    loads = [
        pltpu.make_async_copy(proj_in, proj.at[ds(z * p_rows, p_rows)], local_sem.at[0]),
        pltpu.make_async_copy(rows_in, rows, local_sem.at[1]),
        pltpu.make_async_copy(head_in, head.at[ds(z * h_rows, h_rows)], local_sem.at[2]),
    ]
    for load in loads:
        load.start()
    barrier = pltpu.get_barrier_semaphore()
    for peer in peers:
        pl.semaphore_signal(barrier, inc=1, device_id=peer, device_id_type=pl.DeviceIdType.MESH)
    pl.semaphore_wait(barrier, len(peers))

    proj_t.begin(proj_in)
    gains[z] = jnp.broadcast_to(gain_in[...].astype(f32).reshape(1, h_rows), (8, h_rows))
    gain_copies = [send(gains.at[z], gains.at[z], z_peer(d)) for d in range(1, nz)]
    near = jnp.minimum(z, nz - 1 - z)
    sources = []
    for j in range(nz - 1):
        both = j < 2 * near
        dist = jnp.where(both, j // 2 + 1, j - near + 1)
        down = jnp.where(both, j % 2 == 0, z > nz - 1 - z)
        sources.append(jnp.where(down, z - dist, z + dist))
    items = [(proj_t, zs) for zs in sources] + [(head_t[q], zs) for zs in sources for q in range(halves)]
    for load in loads:
        load.wait()

    def project(zs, fresh):
        depth = ds(zs * p_rows, p_rows)

        @pl.loop(0, slots)
        def _(p):
            at = ds(p * pair_rows, pair_rows)
            part = jnp.dot(rows[at, depth], proj[depth, :], preferred_element_type=f32)
            acc[at, :] = part if fresh else acc[at, :] + part

    def score(zs, q, fresh):
        depth = ds(zs * h_rows, h_rows)
        cols = slice(q * piece, (q + 1) * piece)

        @pl.loop(0, slots)
        def _(p):
            at = ds(p * pair_rows, pair_rows)
            part = jnp.dot(normed[at, depth], head[depth, cols], preferred_element_type=f32)
            logits[at, cols] = part if fresh else logits[at, cols] + part

    def normalise():
        @pl.loop(0, slots * 2)
        def _(b):
            at = ds(b * frames, frames)
            kept = acc[at, :].astype(bf16)
            projected[at, :] = kept
            flat = kept.astype(f32)
            inv = lax.rsqrt(jnp.mean(flat * flat, axis=1, keepdims=True) + norm_eps)
            inverse[at, :] = inv
            for s in range(nz):
                cols = slice(s * h_rows, (s + 1) * h_rows)
                part = flat[:, cols] * inv * gains[s, 0:1, :]
                normed[at, cols] = part.astype(bf16)
                normed_t[cols, at] = jnp.transpose(part).astype(bf16)

    stage2, stage3, stage4 = {}, {}, {}
    for t in range(len(items) + 3):
        if t < len(items):
            tensor, zs = items[t]
            stage2[t] = tensor.second(zs, True)
        if t == 0:
            for half in head_t:
                half.begin(head_in)
            project(z, True)
        if 0 <= t - 1 < len(items):
            tensor, zs = items[t - 1]
            stage3[t - 1] = tensor.third(zs, stage2[t - 1])
        if 0 <= t - 2 < len(items):
            tensor, zs = items[t - 2]
            stage4[t - 2] = tensor.fourth(zs, stage3[t - 2])
        if 0 <= t - 3 < len(items):
            tensor, zs = items[t - 3]
            stage4[t - 3].wait_recv()
            if tensor is proj_t:
                project(zs, False)
                if t - 3 == nz - 2:
                    for copy in gain_copies:
                        copy.wait_recv()
                    normalise()
            else:
                if t - 3 < nz - 1 + halves:
                    score(z, tensor.index - 1, True)
                score(zs, tensor.index - 1, False)

    small[...] = jnp.zeros_like(small)

    @pl.loop(0, slots)
    def _(p):
        token = lax.broadcasted_iota(jnp.int32, (frames, vocab), 1)
        frame = lax.broadcasted_iota(jnp.int32, (frames, 1), 0)
        scores, sums, valids, sizes, columns = [], [], [], [], []
        for b in range(2):
            at = ds(p * pair_rows + b * frames, frames)
            values = logits[at, :]
            highest = jnp.max(values, axis=1, keepdims=True)
            powers = jnp.exp(values - highest)
            total = jnp.sum(powers, axis=1, keepdims=True)
            line = codes[0, 0, p, b : b + 1, :].astype(f32)
            column = jnp.transpose(jnp.broadcast_to(line, (frames, frames)))[:, 0:1].astype(jnp.int32)
            picked = jnp.sum(jnp.where(token == column, values, 0.0), axis=1, keepdims=True)
            logits[at, :] = powers
            held = lengths[0, 0, b : b + 1, :].astype(f32)
            slot = lax.broadcasted_iota(jnp.int32, (1, slots), 1)
            size = jnp.sum(jnp.where(slot == p, held, 0.0), axis=1, keepdims=True)
            valid = (frame.astype(f32) < size).astype(f32)
            logp = picked - (highest + jnp.log(total))
            scores.append(jnp.sum(logp * valid, axis=0, keepdims=True) / size)
            sums.append(total)
            columns.append(column)
            valids.append(valid)
            sizes.append(size)
        sign = jnp.where(labels[p] == 0, 1.0, -1.0).astype(f32)
        live = jnp.where(p < counts[0], 1.0, 0.0).astype(f32)
        margin = margin_scale * (sign * (scores[0] - scores[1]) - ratios[p])
        soft = jnp.maximum(-margin, 0.0) + jnp.log1p(jnp.exp(-jnp.abs(margin)))
        small[:, dim:] += jnp.broadcast_to(soft * live, (small.shape[0], small.shape[1] - dim))
        slope = -jax.nn.sigmoid(-margin) * live
        for b in range(2):
            at = ds(p * pair_rows + b * frames, frames)
            weight = (margin_scale if b == 0 else -margin_scale) * sign * slope / sizes[b]
            coeff = weight * valids[b]
            hot = jnp.where(token == columns[b], coeff, 0.0)
            dlogits[at, :] = (hot - (coeff / sums[b]) * logits[at, :]).astype(bf16)

    rx, cy = h_rows // 2 // nx, piece // 2 // ny
    half_rows, half_cols = h_rows // 2, piece // 2
    tile = min(512, half_cols)
    moves = [(d, q) for d in list(range(1, nz)) + [0] for q in range(halves)]
    blocks = len(moves)
    one, two_x, two_y, three_x, three_y, z_copies = {}, {}, {}, {}, {}, {}

    def head_block(k):
        rows_at = ds(shift(z, moves[k][0], nz) * h_rows, h_rows)
        base = moves[k][1] * piece

        @pl.loop(0, piece // tile)
        def _(j):
            term[k, :, ds(j * tile, tile)] = jnp.dot(
                normed_t[rows_at, :], dlogits[:, ds(base + j * tile, tile)], preferred_element_type=f32
            ).astype(bf16)

        one[k] = send(term.at[k, :, ds((1 - core) * half_cols, half_cols)], r1.at[k], mate)

    def sum_mates(k):
        one[k].wait_recv()
        mine = term[k, :, ds(core * half_cols, half_cols)].astype(f32)
        s1[k] = (mine + r1[k].astype(f32)).astype(bf16)
        for d in range(1, nx):
            two_x[k, d] = send(s1.at[k, ds(shift(x, d, nx) * rx, rx), :], ra0.at[k, d - 1], x_peer(d))
        for d in range(1, ny):
            two_y[k, d] = send(
                s1.at[k, ds(half_rows, half_rows), ds(shift(y, d, ny) * cy, cy)],
                ra1.at[k, d - 1], y_peer(d),
            )

    def sum_first(k):
        for d in range(1, nx):
            two_x[k, d].wait_recv()
        total = s1[k, ds(x * rx, rx), :].astype(f32)
        for d in range(1, nx):
            total = total + ra0[k, d - 1].astype(f32)
        s2a[k] = total.astype(bf16)
        for d in range(1, ny):
            three_y[k, d] = send(s2a.at[k, :, ds(shift(y, d, ny) * cy, cy)], rb0.at[k, d - 1], y_peer(d))
        for d in range(1, ny):
            two_y[k, d].wait_recv()
        total = s1[k, half_rows:, ds(y * cy, cy)].astype(f32)
        for d in range(1, ny):
            total = total + ra1[k, d - 1].astype(f32)
        s2b[k] = total.astype(bf16)
        for d in range(1, nx):
            three_x[k, d] = send(s2b.at[k, ds(shift(x, d, nx) * rx, rx), :], rb1.at[k, d - 1], x_peer(d))

    def sum_second(k):
        for d in range(1, ny):
            three_y[k, d].wait_recv()
        total = s2a[k, :, ds(y * cy, cy)].astype(f32)
        for d in range(1, ny):
            total = total + rb0[k, d - 1].astype(f32)
        s3[k, :rx, :] = total.astype(bf16)
        for d in range(1, nx):
            three_x[k, d].wait_recv()
        total = s2b[k, ds(x * rx, rx), :].astype(f32)
        for d in range(1, nx):
            total = total + rb1[k, d - 1].astype(f32)
        s3[k, rx:, :] = total.astype(bf16)
        d, q = moves[k]
        if d:
            z_copies[d, q] = send(s3.at[k], r3.at[(d - 1) * halves + q], z_peer(d))

    def gain_block(p):
        at = slice(p * frames, (p + 1) * frames)
        dnormed = lax.dot_general(
            dlogits[at, :], head[...], (((1,), (1,)), ((), ())), preferred_element_type=f32
        )
        part = jnp.sum(dnormed * (projected[at, :].astype(f32) * inverse[at, :]), axis=0, keepdims=True)
        small[:, :dim] += jnp.broadcast_to(part, (small.shape[0], dim))

    def finish_block(q):
        total = s3[blocks - halves + q].astype(f32)
        for d in range(1, nz):
            z_copies[d, q].wait_recv()
            total = total + r3[(d - 1) * halves + q].astype(f32)
        for h in range(2):
            gather[out_t[q].box(h, x, y)] = total[h * rx : (h + 1) * rx, :].astype(bf16)

    def share(buffer, value, mine, n, peer):
        buffer[mine] = value
        return [send(buffer.at[mine], buffer.at[mine], peer(d)) for d in range(1, n)]

    def collect(buffer, copies, n):
        for copy in copies:
            copy.wait_recv()
        total = buffer[0]
        for i in range(1, n):
            total = total + buffer[i]
        return total

    last2, last3, last4 = {}, {}, {}
    small_copies = None
    for t in range(blocks + 5):
        if t < blocks:
            head_block(t)
        if 0 <= t - 1 < blocks:
            sum_mates(t - 1)
        if 0 <= t - 2 < blocks:
            sum_first(t - 2)
        if 0 <= t - 3 < blocks:
            sum_second(t - 3)
        q = t - 3 - (blocks - halves)
        if 0 <= q < halves:
            finish_block(q)
            last2[q] = out_t[q].second(0, False)
        if 0 <= q - 1 < halves:
            last3[q - 1] = out_t[q - 1].third(0, last2[q - 1])
        if 0 <= q - 2 < halves:
            last4[q - 2] = out_t[q - 2].fourth(0, last3[q - 2])
        if 0 <= t - 2 < min(slots * 2, blocks - 1):
            gain_block(t - 2)
        if t == blocks:
            for p in range(blocks - 1, slots * 2):
                gain_block(p)
            small_copies = share(sum_z, small[...], z, nz, z_peer)
        if t == blocks + 2:
            value = collect(sum_z, small_copies, nz)
            small_copies = share(sum_w, value, w, wide, w_peer)
    stores = []
    for q in range(halves):
        mine = ds(q * piece + core * half_cols, half_cols)
        stores.append(pltpu.make_async_copy(gather.at[:, mine], grad_out.at[:, mine], local_sem.at[q]))
        stores[q].start()
    value = collect(sum_w, small_copies, wide)
    small[...] = value
    loss_out[...] = value[0:1, dim : dim + 1] / pair_total
    gain_out[...] = small[0:1, ds(z * h_rows, h_rows)]
    for q in range(halves):
        last4[q].wait_recv()
        other = ds(q * piece + (1 - core) * half_cols, half_cols)
        stores.append(
            pltpu.make_async_copy(gather.at[:, other], grad_out.at[:, other], local_sem.at[halves + q])
        )
        stores[halves + q].start()
    for store in stores:
        store.wait()
    for copy in started:
        copy.wait_send()
    proj_t.finish(proj_in, sources)
    for half in head_t:
        half.finish(head_in, sources)


def on_device(
    thinker_rows, codec_ids, block_lengths, chosen_label, ref_logratio, pair_count,
    proj_weight, norm_gain, head_weight,
):
    slots, frames, width = thinker_rows.shape[2], thinker_rows.shape[4], thinker_rows.shape[5]
    dim, vocab = proj_weight.shape[1], head_weight.shape[1]
    wide, nz = lax.axis_size("wide"), lax.axis_size("narrow")
    ny, nx = plane_of(wide)
    count = slots * 2 * frames
    hold = (slots + 1) // 2
    h_rows = dim // nz
    piece = vocab // halves
    rx, cy = h_rows // 2 // nx, piece // 2 // ny
    half = piece // 2
    nb = nz * halves
    n = copy_count(nx, ny, nz)
    vmem, smem = pl.BlockSpec(memory_space=pltpu.VMEM), pl.BlockSpec(memory_space=pltpu.SMEM)
    hbm = pl.BlockSpec(memory_space=pl.ANY)
    line = (8, dim + 128)
    scratch = [
        pltpu.VMEM((count, width), bf16),
        pltpu.VMEM((width, dim), bf16),
        pltpu.VMEM((dim, vocab), bf16),
        pltpu.VMEM((nz, 8, h_rows), f32),
        pltpu.VMEM((count, dim), f32),
        pltpu.VMEM((count, dim), bf16),
        pltpu.VMEM((count, 1), f32),
        pltpu.VMEM((count, dim), bf16),
        pltpu.VMEM((dim, count), bf16),
        pltpu.VMEM((count, vocab), f32),
        pltpu.VMEM((count, vocab), bf16),
        pltpu.VMEM((nb, h_rows, piece), bf16),
        pltpu.VMEM((nb, h_rows, half), bf16),
        pltpu.VMEM((nb, h_rows, half), bf16),
        pltpu.VMEM((nb, nx - 1, rx, half), bf16),
        pltpu.VMEM((nb, ny - 1, h_rows // 2, cy), bf16),
        pltpu.VMEM((nb, rx, half), bf16),
        pltpu.VMEM((nb, h_rows // 2, cy), bf16),
        pltpu.VMEM((nb, ny - 1, rx, cy), bf16),
        pltpu.VMEM((nb, nx - 1, rx, cy), bf16),
        pltpu.VMEM((nb, 2 * rx, cy), bf16),
        pltpu.VMEM((nb - halves, 2 * rx, cy), bf16),
        pltpu.VMEM((h_rows, vocab), bf16),
        pltpu.VMEM(line, f32),
        pltpu.VMEM((nz,) + line, f32),
        pltpu.VMEM((wide,) + line, f32),
        pltpu.SemaphoreType.DMA((4,)),
        pltpu.SemaphoreType.DMA((n,)),
        pltpu.SemaphoreType.DMA((n,)),
        pltpu.SemaphoreType.DMA((1 + halves, 2, nz + 1)),
        pltpu.SemaphoreType.DMA((1 + halves, 2, nz)),
    ]
    loss, grad_head, grad_gain = pl.pallas_call(
        functools.partial(
            kernel, ny, nx, nz, slots, frames, width, dim, vocab, float(wide * nz * hold)
        ),
        out_shape=[
            jax.ShapeDtypeStruct((1, 1), f32),
            jax.ShapeDtypeStruct((h_rows, vocab), bf16),
            jax.ShapeDtypeStruct((1, h_rows), f32),
        ],
        in_specs=[smem, smem, smem, vmem, vmem, vmem, hbm, hbm, hbm],
        out_specs=[vmem, hbm, vmem],
        scratch_shapes=scratch,
        compiler_params=pltpu.CompilerParams(
            collective_id=0, has_side_effects=True, vmem_limit_bytes=58 * 1024 * 1024
        ),
        cost_estimate=pl.CostEstimate(
            flops=8 * count * width * dim, bytes_accessed=count * width * 8, transcendentals=count * vocab
        ),
    )(
        chosen_label[0, 0],
        pair_count[0],
        ref_logratio[0, 0],
        jnp.swapaxes(block_lengths, 2, 3),
        codec_ids,
        norm_gain,
        thinker_rows.reshape(count, width),
        proj_weight,
        head_weight,
    )
    return loss[0, 0], grad_head.astype(f32), grad_gain[0]


def solution(mesh):
    in_specs = (
        P("wide", "narrow", None, None, None, None),
        P("wide", "narrow", None, None, None),
        P("wide", "narrow", None, None),
        P("wide", "narrow", None),
        P("wide", "narrow", None),
        P("wide", "narrow"),
        P("narrow", None),
        P("narrow"),
        P("narrow", None),
    )
    out_specs = (P(), P("narrow", None), P("narrow"))
    return jax.shard_map(
        on_device, mesh=mesh, in_specs=in_specs, out_specs=out_specs, check_vma=False
    )
```

```python
import functools

import jax
import jax.numpy as jnp
from jax import lax
from jax.experimental import pallas as pl
from jax.experimental.pallas import tpu as pltpu
from jax.sharding import PartitionSpec as P

norm_eps = 1e-06
margin_scale = 2.0
f32 = jnp.float32
bf16 = jnp.bfloat16


def plane_of(wide):
    chips = wide // 2
    rows = 1
    while (rows * 2) * (rows * 2) <= chips:
        rows *= 2
    return rows, chips // rows


def spread_count(nx, ny):
    return 2 * (nx - 1) + 2 * (ny - 1) + 2 * (nx - 1) * (ny - 1) + 1


def copy_count(nx, ny, nz):
    weights = 2 * (nz - 1) * spread_count(nx, ny) + (nz - 1)
    sums = nz * (1 + 2 * (nx - 1) + 2 * (ny - 1)) + (nz - 1)
    small = 1 + (nx - 1) + (ny - 1) + (nz - 1)
    return weights + sums + spread_count(nx, ny) + small


def kernel(
    ny, nx, nz, slots, frames, width, dim, vocab, pair_total,
    labels, counts, ratios, lengths, codes, gain_in,
    rows_in, proj_in, head_in,
    loss_out, grad_out, gain_out,
    rows, proj, head, gains, acc, projected, inverse, normed, normed_t, logits, dlogits,
    term, r1, s1, ra0, ra1, s2a, s2b, rb0, rb1, s3, r3, gather,
    small, sum_c, sum_x, sum_y, sum_z, scores, sums, columns,
    local_sem, send_sem, recv_sem, line_send, line_recv,
):
    w = lax.axis_index("wide")
    z = lax.axis_index("narrow")
    core = lax.rem(w, 2)
    chip = lax.div(w, 2)
    x = lax.rem(chip, nx)
    y = lax.div(chip, nx)
    pair_rows = 2 * frames
    total_rows = slots * pair_rows

    def wide_at(yy, xx, cc):
        return (yy * nx + xx) * 2 + cc

    def shift(i, d, n):
        return lax.rem(i + d, n)

    def x_peer(d):
        return {"wide": wide_at(y, shift(x, d, nx), core), "narrow": z}

    def y_peer(d):
        return {"wide": wide_at(shift(y, d, ny), x, core), "narrow": z}

    def z_peer(d):
        return {"wide": w, "narrow": shift(z, d, nz)}

    mate = {"wide": wide_at(y, x, 1 - core), "narrow": z}
    peers = [mate]
    peers += [x_peer(d) for d in range(1, nx)]
    peers += [y_peer(d) for d in range(1, ny)]
    peers += [z_peer(d) for d in range(1, nz)]

    started = []

    def send(src, dst, device):
        at = len(started)
        copy = pltpu.make_async_remote_copy(
            src_ref=src,
            dst_ref=dst,
            send_sem=send_sem.at[at],
            recv_sem=recv_sem.at[at],
            device_id=device,
            device_id_type=pl.DeviceIdType.MESH,
        )
        copy.start()
        started.append(copy)
        return copy

    def ds(start, size):
        return pl.ds(start if isinstance(start, int) else pl.multiple_of(start, size), size)

    class Tensor:
        def __init__(self, full, shard_rows):
            self.full = full
            self.rows = shard_rows
            self.cols = full.shape[1]
            self.part = shard_rows // 2 // nx
            self.wide = self.cols // 2 // ny

        def box(self, h, xx, yy):
            row = h * (self.rows // 2) + xx * self.part
            return ds(row, self.part), ds((core * ny + yy) * self.wide, self.wide)

        def region(self, zs, h, xx, yy):
            row = zs * self.rows + h * (self.rows // 2) + xx * self.part
            return self.full.at[ds(row, self.part), ds((core * ny + yy) * self.wide, self.wide)]

        def line(self, src, zs, h, send_at, target):
            which = 0 if self is proj_t else 1
            here = self.region(zs, h, x, y)
            return pltpu.make_async_remote_copy(
                src_ref=here if src is None else src.at[self.box(h, x, y)],
                dst_ref=here,
                send_sem=line_send.at[which, h, send_at],
                recv_sem=line_recv.at[which, h, zs],
                device_id={"wide": w, "narrow": target},
                device_id_type=pl.DeviceIdType.MESH,
            )

        def begin(self, src):
            for h in range(2):
                @pl.when(z + 1 < nz)
                def _():
                    self.line(src, z, h, z, z + 1).start()

                @pl.when(z > 0)
                def _():
                    self.line(src, z, h, nz, z - 1).start()

        def arrive(self, zs, h):
            self.line(None, zs, h, zs, lax.rem(z + 1, nz)).wait_recv()

            @pl.when((zs < z) & (z + 1 < nz))
            def _():
                self.line(None, zs, h, zs, z + 1).start()

            @pl.when((zs > z) & (z > 0))
            def _():
                self.line(None, zs, h, zs, z - 1).start()

        def finish(self, src, sources):
            for h in range(2):
                @pl.when(z + 1 < nz)
                def _():
                    self.line(src, z, h, z, z + 1).wait_send()

                @pl.when(z > 0)
                def _():
                    self.line(src, z, h, nz, z - 1).wait_send()

                for zs in sources:
                    @pl.when((zs < z) & (z + 1 < nz))
                    def _():
                        self.line(None, zs, h, zs, z + 1).wait_send()

                    @pl.when((zs > z) & (z > 0))
                    def _():
                        self.line(None, zs, h, zs, z - 1).wait_send()

        def second(self, zs, arrives):
            out = ({}, {})
            for h in range(2):
                if arrives:
                    self.arrive(zs, h)
                mine = self.region(zs, h, x, y)
                for d in range(1, nx):
                    out[0][d, h] = send(mine, mine, x_peer(d))
                for d in range(1, ny):
                    out[1][d, h] = send(mine, mine, y_peer(d))
            return out

        def third(self, zs, out):
            later = []
            for d in range(1, nx):
                out[0][d, 0].wait_recv()
                got = self.region(zs, 0, shift(x, nx - d, nx), y)
                later += [send(got, got, y_peer(e)) for e in range(1, ny)]
            for d in range(1, ny):
                out[1][d, 1].wait_recv()
                got = self.region(zs, 1, x, shift(y, ny - d, ny))
                later += [send(got, got, x_peer(e)) for e in range(1, nx)]
            later += [out[0][d, 1] for d in range(1, nx)]
            later += [out[1][d, 0] for d in range(1, ny)]
            return later

        def fourth(self, zs, later):
            for copy in later:
                copy.wait_recv()
            half = self.full.at[ds(zs * self.rows, self.rows), ds(core * (self.cols // 2), self.cols // 2)]
            return send(half, half, mate)

    p_rows, h_rows = width // nz, dim // nz
    proj_t, head_t = Tensor(proj, p_rows), Tensor(head, h_rows)
    out_t = Tensor(gather, h_rows)

    loads = [
        pltpu.make_async_copy(proj_in, proj.at[ds(z * p_rows, p_rows)], local_sem.at[0]),
        pltpu.make_async_copy(rows_in, rows, local_sem.at[1]),
        pltpu.make_async_copy(head_in, head.at[ds(z * h_rows, h_rows)], local_sem.at[2]),
    ]
    for load in loads:
        load.start()
    barrier = pltpu.get_barrier_semaphore()
    for peer in peers:
        pl.semaphore_signal(barrier, inc=1, device_id=peer, device_id_type=pl.DeviceIdType.MESH)
    pl.semaphore_wait(barrier, len(peers))

    proj_t.begin(proj_in)
    gains[z] = jnp.broadcast_to(gain_in[...].astype(f32).reshape(1, h_rows), (8, h_rows))
    gain_copies = [send(gains.at[z], gains.at[z], z_peer(d)) for d in range(1, nz)]
    near = jnp.minimum(z, nz - 1 - z)
    sources = []
    for j in range(nz - 1):
        both = j < 2 * near
        dist = jnp.where(both, j // 2 + 1, j - near + 1)
        down = jnp.where(both, j % 2 == 0, z > nz - 1 - z)
        sources.append(jnp.where(down, z - dist, z + dist))
    items = [(proj_t, zs) for zs in sources] + [(head_t, zs) for zs in sources]
    for load in loads:
        load.wait()

    def project(zs, fresh):
        depth = ds(zs * p_rows, p_rows)

        @pl.loop(0, dim // 512)
        def _(j):
            cols = ds(j * 512, 512)

            @pl.loop(0, slots)
            def _(p):
                at = ds(p * pair_rows, pair_rows)
                part = jnp.dot(rows[at, depth], proj[depth, cols], preferred_element_type=f32)
                acc[at, cols] = part if fresh else acc[at, cols] + part

    def score(zs, fresh):
        depth = ds(zs * h_rows, h_rows)

        @pl.loop(0, vocab // 1024)
        def _(j):
            cols = ds(j * 1024, 1024)

            @pl.loop(0, slots)
            def _(p):
                at = ds(p * pair_rows, pair_rows)
                part = jnp.dot(normed[at, depth], head[depth, cols], preferred_element_type=f32)
                logits[at, cols] = part if fresh else logits[at, cols] + part

    def normalise():
        @pl.loop(0, slots * 2)
        def _(b):
            at = ds(b * frames, frames)
            kept = acc[at, :].astype(bf16)
            projected[at, :] = kept
            flat = kept.astype(f32)
            inv = lax.rsqrt(jnp.mean(flat * flat, axis=1, keepdims=True) + norm_eps)
            inverse[at, :] = inv
            for s in range(nz):
                cols = slice(s * h_rows, (s + 1) * h_rows)
                part = flat[:, cols] * inv * gains[s, 0:1, :]
                normed[at, cols] = part.astype(bf16)
                normed_t[cols, at] = jnp.transpose(part).astype(bf16)

    stage2, stage3, stage4 = {}, {}, {}
    for t in range(len(items) + 3):
        if t < len(items):
            tensor, zs = items[t]
            stage2[t] = tensor.second(zs, True)
        if t == 0:
            head_t.begin(head_in)
            project(z, True)
        if 0 <= t - 1 < len(items):
            tensor, zs = items[t - 1]
            stage3[t - 1] = tensor.third(zs, stage2[t - 1])
        if 0 <= t - 2 < len(items):
            tensor, zs = items[t - 2]
            stage4[t - 2] = tensor.fourth(zs, stage3[t - 2])
        if 0 <= t - 3 < len(items):
            tensor, zs = items[t - 3]
            stage4[t - 3].wait_recv()
            if tensor is proj_t:
                project(zs, False)
                if t - 3 == nz - 2:
                    for copy in gain_copies:
                        copy.wait_recv()
                    normalise()
                    score(z, True)
            else:
                score(zs, False)

    small[...] = jnp.zeros_like(small)

    @pl.loop(0, slots)
    def _(p):
        token = lax.broadcasted_iota(jnp.int32, (frames, vocab), 1)
        frame = lax.broadcasted_iota(jnp.int32, (frames, 1), 0)

        def size_of(b):
            held = lengths[0, 0, pl.ds(b, 1), :].astype(f32)
            slot = lax.broadcasted_iota(jnp.int32, (1, slots), 1)
            return jnp.sum(jnp.where(slot == p, held, 0.0), axis=1, keepdims=True)

        @pl.loop(0, 2)
        def _(b):
            at = ds(p * pair_rows + b * frames, frames)
            values = logits[at, :]
            highest = jnp.max(values, axis=1, keepdims=True)
            powers = jnp.exp(values - highest)
            total = jnp.sum(powers, axis=1, keepdims=True)
            line = codes[0, 0, p, pl.ds(b, 1), :].astype(f32)
            column = jnp.transpose(jnp.broadcast_to(line, (frames, frames)))[:, 0:1].astype(jnp.int32)
            picked = jnp.sum(jnp.where(token == column, values, 0.0), axis=1, keepdims=True)
            logits[at, :] = powers
            size = size_of(b)
            valid = (frame.astype(f32) < size).astype(f32)
            logp = picked - (highest + jnp.log(total))
            result = jnp.sum(logp * valid, axis=0, keepdims=True) / size
            scores[b] = jnp.broadcast_to(result, (8, 128))
            sums[at, :] = total
            columns[at, :] = column

        sign = jnp.where(labels[p] == 0, 1.0, -1.0).astype(f32)
        live = jnp.where(p < counts[0], 1.0, 0.0).astype(f32)
        margin = margin_scale * (sign * (scores[0, 0:1, 0:1] - scores[1, 0:1, 0:1]) - ratios[p])
        soft = jnp.maximum(-margin, 0.0) + jnp.log1p(jnp.exp(-jnp.abs(margin)))
        small[:, dim:] += jnp.broadcast_to(soft * live, (small.shape[0], small.shape[1] - dim))
        slope = -jax.nn.sigmoid(-margin) * live

        @pl.loop(0, 2)
        def _(b):
            at = ds(p * pair_rows + b * frames, frames)
            size = size_of(b)
            valid = (frame.astype(f32) < size).astype(f32)
            side = jnp.where(b == 0, margin_scale, -margin_scale).astype(f32)
            coeff = (side * sign * slope / size) * valid
            hot = jnp.where(token == columns[at, :], coeff, 0.0)
            dlogits[at, :] = (hot - (coeff / sums[at, :]) * logits[at, :]).astype(bf16)

    rx, cy = h_rows // 2 // nx, vocab // 2 // ny
    half_rows, half_cols = h_rows // 2, vocab // 2
    tile = min(512, half_cols)
    moves = list(range(1, nz)) + [0]
    one, two_x, two_y, three_x, three_y, z_copies = {}, {}, {}, {}, {}, {}

    def head_block(k):
        rows_at = ds(shift(z, moves[k], nz) * h_rows, h_rows)

        @pl.loop(0, vocab // tile)
        def _(j):
            cols = ds(j * tile, tile)
            term[k, :, cols] = jnp.dot(
                normed_t[rows_at, :], dlogits[:, cols], preferred_element_type=f32
            ).astype(bf16)

        one[k] = send(term.at[k, :, ds((1 - core) * half_cols, half_cols)], r1.at[k], mate)

    def sum_mates(k):
        one[k].wait_recv()

        @pl.loop(0, 4)
        def _(i):
            at = ds(i * (h_rows // 4), h_rows // 4)
            mine = term[k, at, ds(core * half_cols, half_cols)].astype(f32)
            s1[k, at, :] = (mine + r1[k, at, :].astype(f32)).astype(bf16)

        for d in range(1, nx):
            two_x[k, d] = send(s1.at[k, ds(shift(x, d, nx) * rx, rx), :], ra0.at[k, d - 1], x_peer(d))
        for d in range(1, ny):
            two_y[k, d] = send(
                s1.at[k, ds(half_rows, half_rows), ds(shift(y, d, ny) * cy, cy)],
                ra1.at[k, d - 1], y_peer(d),
            )

    def sum_first(k):
        for d in range(1, nx):
            two_x[k, d].wait_recv()
        total = s1[k, ds(x * rx, rx), :].astype(f32)
        for d in range(1, nx):
            total = total + ra0[k, d - 1].astype(f32)
        s2a[k] = total.astype(bf16)
        for d in range(1, ny):
            three_y[k, d] = send(s2a.at[k, :, ds(shift(y, d, ny) * cy, cy)], rb0.at[k, d - 1], y_peer(d))
        for d in range(1, ny):
            two_y[k, d].wait_recv()
        total = s1[k, half_rows:, ds(y * cy, cy)].astype(f32)
        for d in range(1, ny):
            total = total + ra1[k, d - 1].astype(f32)
        s2b[k] = total.astype(bf16)
        for d in range(1, nx):
            three_x[k, d] = send(s2b.at[k, ds(shift(x, d, nx) * rx, rx), :], rb1.at[k, d - 1], x_peer(d))

    def sum_second(k):
        for d in range(1, ny):
            three_y[k, d].wait_recv()
        total = s2a[k, :, ds(y * cy, cy)].astype(f32)
        for d in range(1, ny):
            total = total + rb0[k, d - 1].astype(f32)
        s3[k, :rx, :] = total.astype(bf16)
        for d in range(1, nx):
            three_x[k, d].wait_recv()
        total = s2b[k, ds(x * rx, rx), :].astype(f32)
        for d in range(1, nx):
            total = total + rb1[k, d - 1].astype(f32)
        s3[k, rx:, :] = total.astype(bf16)
        if moves[k]:
            z_copies[moves[k]] = send(s3.at[k], r3.at[moves[k] - 1], z_peer(moves[k]))

    def gain_block(p):
        at = slice(p * pair_rows, (p + 1) * pair_rows)

        @pl.loop(0, dim // 256)
        def _(j):
            cols = ds(j * 256, 256)
            dnormed = lax.dot_general(
                dlogits[at, :], head[cols, :], (((1,), (1,)), ((), ())), preferred_element_type=f32
            )
            part = dnormed * (projected[at, cols].astype(f32) * inverse[at, :])
            small[:, cols] += jnp.broadcast_to(jnp.sum(part, axis=0, keepdims=True), (small.shape[0], 256))

    def share(buffer, value, mine, n, peer):
        buffer[mine] = value
        return [send(buffer.at[mine], buffer.at[mine], peer(d)) for d in range(1, n)]

    def collect(buffer, copies, n):
        for copy in copies:
            copy.wait_recv()
        total = buffer[0]
        for i in range(1, n):
            total = total + buffer[i]
        return total

    small_copies = None
    for t in range(max(nz + 3, slots + 4)):
        if t < nz:
            head_block(t)
        if 0 <= t - 1 < nz:
            sum_mates(t - 1)
        if 0 <= t - 2 < nz:
            sum_first(t - 2)
        if 0 <= t - 3 < nz:
            sum_second(t - 3)
        if 0 <= t - 2 < slots:
            gain_block(t - 2)
        if t == slots + 1:
            small_copies = share(sum_c, small[...], core, 2, lambda d: mate)
        if t == slots + 2:
            value = collect(sum_c, small_copies, 2)
            small_copies = share(sum_x, value, x, nx, x_peer)
        if t == slots + 3:
            value = collect(sum_x, small_copies, nx)
            small_copies = share(sum_y, value, y, ny, y_peer)

    total = s3[nz - 1].astype(f32)
    for d in range(1, nz):
        z_copies[d].wait_recv()
        total = total + r3[d - 1].astype(f32)
    for h in range(2):
        gather[out_t.box(h, x, y)] = total[h * rx : (h + 1) * rx, :].astype(bf16)
    last = out_t.second(0, False)
    value = collect(sum_y, small_copies, ny)
    small_copies = share(sum_z, value, z, nz, z_peer)
    last = out_t.fourth(0, out_t.third(0, last))
    mine = ds(core * half_cols, half_cols)
    stores = [pltpu.make_async_copy(gather.at[:, mine], grad_out.at[:, mine], local_sem.at[0])]
    stores[0].start()
    value = collect(sum_z, small_copies, nz)
    small[...] = value
    loss_out[...] = value[0:1, dim : dim + 1] / pair_total
    gain_out[...] = small[0:1, ds(z * h_rows, h_rows)]
    last.wait_recv()
    other = ds((1 - core) * half_cols, half_cols)
    stores.append(pltpu.make_async_copy(gather.at[:, other], grad_out.at[:, other], local_sem.at[1]))
    stores[1].start()
    for store in stores:
        store.wait()
    for copy in started:
        copy.wait_send()
    proj_t.finish(proj_in, sources)
    head_t.finish(head_in, sources)


def on_device(
    thinker_rows, codec_ids, block_lengths, chosen_label, ref_logratio, pair_count,
    proj_weight, norm_gain, head_weight,
):
    slots, frames, width = thinker_rows.shape[2], thinker_rows.shape[4], thinker_rows.shape[5]
    dim, vocab = proj_weight.shape[1], head_weight.shape[1]
    wide, nz = lax.axis_size("wide"), lax.axis_size("narrow")
    ny, nx = plane_of(wide)
    count = slots * 2 * frames
    hold = (slots + 1) // 2
    h_rows = dim // nz
    rx, cy = h_rows // 2 // nx, vocab // 2 // ny
    half = vocab // 2
    n = copy_count(nx, ny, nz)
    vmem, smem = pl.BlockSpec(memory_space=pltpu.VMEM), pl.BlockSpec(memory_space=pltpu.SMEM)
    hbm = pl.BlockSpec(memory_space=pl.ANY)
    line = (8, dim + 128)
    scratch = [
        pltpu.VMEM((count, width), bf16),
        pltpu.VMEM((width, dim), bf16),
        pltpu.VMEM((dim, vocab), bf16),
        pltpu.VMEM((nz, 8, h_rows), f32),
        pltpu.VMEM((count, dim), f32),
        pltpu.VMEM((count, dim), bf16),
        pltpu.VMEM((count, 1), f32),
        pltpu.VMEM((count, dim), bf16),
        pltpu.VMEM((dim, count), bf16),
        pltpu.VMEM((count, vocab), f32),
        pltpu.VMEM((count, vocab), bf16),
        pltpu.VMEM((nz, h_rows, vocab), bf16),
        pltpu.VMEM((nz, h_rows, half), bf16),
        pltpu.VMEM((nz, h_rows, half), bf16),
        pltpu.VMEM((nz, nx - 1, rx, half), bf16),
        pltpu.VMEM((nz, ny - 1, h_rows // 2, cy), bf16),
        pltpu.VMEM((nz, rx, half), bf16),
        pltpu.VMEM((nz, h_rows // 2, cy), bf16),
        pltpu.VMEM((nz, ny - 1, rx, cy), bf16),
        pltpu.VMEM((nz, nx - 1, rx, cy), bf16),
        pltpu.VMEM((nz, 2 * rx, cy), bf16),
        pltpu.VMEM((nz - 1, 2 * rx, cy), bf16),
        pltpu.VMEM((h_rows, vocab), bf16),
        pltpu.VMEM(line, f32),
        pltpu.VMEM((2,) + line, f32),
        pltpu.VMEM((nx,) + line, f32),
        pltpu.VMEM((ny,) + line, f32),
        pltpu.VMEM((nz,) + line, f32),
        pltpu.VMEM((2, 8, 128), f32),
        pltpu.VMEM((count, 1), f32),
        pltpu.VMEM((count, 1), jnp.int32),
        pltpu.SemaphoreType.DMA((4,)),
        pltpu.SemaphoreType.DMA((n,)),
        pltpu.SemaphoreType.DMA((n,)),
        pltpu.SemaphoreType.DMA((2, 2, nz + 1)),
        pltpu.SemaphoreType.DMA((2, 2, nz)),
    ]
    loss, grad_head, grad_gain = pl.pallas_call(
        functools.partial(
            kernel, ny, nx, nz, slots, frames, width, dim, vocab, float(wide * nz * hold)
        ),
        out_shape=[
            jax.ShapeDtypeStruct((1, 1), f32),
            jax.ShapeDtypeStruct((h_rows, vocab), bf16),
            jax.ShapeDtypeStruct((1, h_rows), f32),
        ],
        in_specs=[smem, smem, smem, vmem, vmem, vmem, hbm, hbm, hbm],
        out_specs=[vmem, hbm, vmem],
        scratch_shapes=scratch,
        compiler_params=pltpu.CompilerParams(
            collective_id=0, has_side_effects=True, vmem_limit_bytes=58 * 1024 * 1024
        ),
        cost_estimate=pl.CostEstimate(
            flops=8 * count * width * dim, bytes_accessed=count * width * 8, transcendentals=count * vocab
        ),
    )(
        chosen_label[0, 0],
        pair_count[0],
        ref_logratio[0, 0],
        jnp.swapaxes(block_lengths, 2, 3),
        codec_ids,
        norm_gain,
        thinker_rows.reshape(count, width),
        proj_weight,
        head_weight,
    )
    return loss[0, 0], grad_head.astype(f32), grad_gain[0]


def solution(mesh):
    in_specs = (
        P("wide", "narrow", None, None, None, None),
        P("wide", "narrow", None, None, None),
        P("wide", "narrow", None, None),
        P("wide", "narrow", None),
        P("wide", "narrow", None),
        P("wide", "narrow"),
        P("narrow", None),
        P("narrow"),
        P("narrow", None),
    )
    out_specs = (P(), P("narrow", None), P("narrow"))
    return jax.shard_map(
        on_device, mesh=mesh, in_specs=in_specs, out_specs=out_specs, check_vma=False
    )
```
